256 devices in a mesh: row: 8 (over z_lo, core), col: 32 (over x, z_hi, y).
Axes of the slice: x: 4, y: 4, z: 8 (z_hi: 2, z_lo: 4; z = z_hi * 4 + z_lo), core: 2. Of those that a mesh axis runs over, the one named last changes fastest.
Arguments:
- features: bfloat16 [65536, 128], P(('row', 'col')), may hold values from -6 to 6
- weight: bfloat16 [128, 256], replicated, may hold values from -0.5 to 0.5
- bias_vector: float32 [256], replicated, may hold values from -3 to 3
- cotangent: bfloat16 [65536, 256], P(('row', 'col')), may hold values from -6 to 6
- degrees: int32 [65536], P(('row', 'col')), may hold values from 1 to 255
- adjacency_tiles: bfloat16 [8, 32, 128, 128, 128], P('row', 'col'), may hold values from 0 to 1, as said below
- tile_positions: int32 [8, 32, 128], P('row', 'col'), may hold values from 0 to 1023, as said below
- tile_counts: int32 [8, 32], P('row', 'col'), may hold values from 16 to 128, as said below
Outputs:
- activations: bfloat16 [65536, 256], P(('row', 'col'))
- grad_features: bfloat16 [65536, 128], P(('row', 'col'))
- grad_weight: float32 [128, 256], replicated
- grad_bias: float32 [256], replicated
The draws below stay inside these ranges and needn't reach their ends.
Inputs may be any that keep to these rules, and one draw needn't show every extreme that they name: `tile_positions`: the first tile_counts[r, c] positions of device (r, c) are distinct; each position q stands for row block q // 16 and column block q % 16 of that device. `tile_counts`: some device has all 128 slots live. `adjacency_tiles`: entries are 0 or 1.
All inputs are finite; a program needn't handle non-finite values.
Results may differ from the reference program's by a relative error of at most 0.015.
Values may be sent and summed in bfloat16 or wider, within the bound.
A program may use at most 128 MiB of HBM per device.

```python
import jax
import jax.numpy as jnp
from jax import lax

F_IN = 128
HID = 256
BLOCK = 128
BPD = 2
TILES_DEV = 128
RBLK = 64
CBLK = 16
NODES = 65536
N_ROW = 8
N_COL = 32


def draw_adjacency_tiles(key, part):
    key = jax.random.fold_in(key, 31)
    values = jax.random.uniform(key, (N_ROW, N_COL, TILES_DEV, BLOCK, BLOCK), jnp.float32)
    return (values < 0.2).astype(jnp.float32).astype(jnp.bfloat16)


def draw_tile_positions(key, part):
    key = jax.random.fold_in(key, 32)
    keys = jax.random.split(key, N_ROW * N_COL)
    chosen = jax.vmap(lambda single: jax.random.permutation(single, RBLK * CBLK)[:TILES_DEV])(keys)
    return chosen.reshape(N_ROW, N_COL, TILES_DEV).astype(jnp.int32)


def draw_tile_counts(key, part):
    key = jax.random.fold_in(key, 33)
    first, second = jax.random.split(key)
    drawn = jax.random.randint(first, (N_ROW * N_COL,), 0, 64, dtype=jnp.int32)
    counts = TILES_DEV // 8 + (TILES_DEV - TILES_DEV // 8) * drawn * drawn // 4032
    fullest = jax.random.randint(second, (), 0, N_ROW * N_COL, dtype=jnp.int32)
    counts = counts.at[fullest].set(TILES_DEV)
    return counts.reshape(N_ROW, N_COL).astype(jnp.int32)


def plant(values, rng, smallest, largest):
    index_at = [jax.random.randint(jax.random.fold_in(rng, axis), (), 0, length) for axis, length in enumerate(values.shape)]
    main_axis = values.shape.index(max(values.shape))
    next_to = index_at[:main_axis] + [(index_at[main_axis] + 1) % values.shape[main_axis]] + index_at[main_axis + 1:]
    return values.at[tuple(index_at)].set(smallest).at[tuple(next_to)].set(largest)


def level_of(key, shape, pieces, least, top_value):
    def one(dim, shards_of):
        steps = jax.random.uniform(jax.random.fold_in(jax.random.fold_in(key, 6), dim), (shards_of,), jnp.float32, least / len(pieces), top_value / len(pieces))
        return jnp.repeat(jnp.exp(steps), shape[dim] // shards_of).reshape((-1,) + (1,) * (len(shape) - dim - 1))

    loudness = one(*pieces[0])
    for cut in pieces[1:]:
        loudness = loudness * one(*cut)
    return loudness


def noise(rng, extent, spread, limit, pieces=(), kind=jnp.bfloat16):
    level = level_of(rng, extent, pieces, -0.22, 0.18) if pieces else 1.0
    values = jax.random.normal(rng, extent, jnp.float32) * spread * level
    return jnp.minimum(jnp.maximum(values, -limit), limit).astype(kind)


def setup_inputs(seed: int = 0) -> dict:
    key_list = jax.random.split(jax.random.key(seed), 9)
    features = noise(key_list[0], (NODES, F_IN), 1.0, 6.0, ((0, 256),))
    weight = noise(key_list[1], (F_IN, HID), F_IN ** -0.5, 0.5)
    bias_vector = noise(key_list[2], (HID,), 0.5, 3.0, (), jnp.float32)
    cotangent = noise(key_list[3], (NODES, HID), 1.0, 6.0, ((0, 256),))
    degrees = plant(jax.random.randint(key_list[4], (NODES,), 1, 256), jax.random.fold_in(key_list[4], 1), 1, 255).astype(jnp.int32)
    adjacency_tiles = draw_adjacency_tiles(jax.random.fold_in(key_list[8], 71), 0)
    tile_positions = draw_tile_positions(jax.random.fold_in(key_list[8], 71), 0)
    tile_counts = draw_tile_counts(jax.random.fold_in(key_list[8], 71), 0)
    return dict(features=features, weight=weight, bias_vector=bias_vector, cotangent=cotangent, degrees=degrees, adjacency_tiles=adjacency_tiles, tile_positions=tile_positions, tile_counts=tile_counts)


def aggregate(source, adjacency_tiles, tile_positions, tile_counts, transposed):
    columns = source.shape[1]
    blocks_all = NODES // BLOCK
    blocked = source.astype(jnp.float32).reshape(blocks_all, BLOCK, columns)
    devices = N_ROW * N_COL
    flat_tiles = adjacency_tiles.reshape(devices, TILES_DEV, BLOCK, BLOCK)
    flat_positions = tile_positions.reshape(devices, TILES_DEV)
    flat_counts = tile_counts.reshape(devices)
    slot_index = jnp.arange(TILES_DEV, dtype=jnp.int32)

    def advance(totals, scan_items):
        tile_data, positions, total_live, device = scan_items
        row_index = device // N_COL
        col_index = device % N_COL
        row_block = positions // CBLK
        col_block = positions % CBLK
        global_rows = (row_index * RBLK + row_block).astype(jnp.int32)
        global_cols = ((col_block // BPD * N_COL + col_index) * BPD + col_block % BPD).astype(jnp.int32)
        active = (slot_index < total_live).astype(jnp.float32)
        tile_values = tile_data.astype(jnp.float32)
        if transposed:
            picked = blocked[global_rows]
            contrib = jnp.einsum('tji,tjf->tif', tile_values, picked, precision=lax.Precision.HIGHEST)
            targets = global_cols
        else:
            picked = blocked[global_cols]
            contrib = jnp.einsum('tij,tjf->tif', tile_values, picked, precision=lax.Precision.HIGHEST)
            targets = global_rows
        contrib = contrib * active[:, None, None]
        return (totals.at[targets].add(contrib), None)
    start = jnp.zeros((blocks_all, BLOCK, columns), jnp.float32)
    totals, _ = lax.scan(advance, start, (flat_tiles, flat_positions, flat_counts, jnp.arange(devices, dtype=jnp.int32)))
    return totals.reshape(NODES, columns)

def reference(features, weight, bias_vector, cotangent, degrees, adjacency_tiles, tile_positions, tile_counts):
    scale_rows = lax.rsqrt(degrees.astype(jnp.float32))[:, None]
    scaled = (scale_rows * features.astype(jnp.float32)).astype(jnp.bfloat16)
    aggregated = aggregate(scaled, adjacency_tiles, tile_positions, tile_counts, False)
    hidden = scale_rows * aggregated
    weight_full = weight.astype(jnp.float32)
    preact = jnp.dot(hidden, weight_full, precision=lax.Precision.HIGHEST) + bias_vector[None, :]
    logistic = jax.nn.sigmoid(preact)
    activations = (preact * logistic).astype(jnp.bfloat16)
    grad_pre = cotangent.astype(jnp.float32) * logistic * (1.0 + preact * (1.0 - logistic))
    grad_bias = lax.optimization_barrier(jnp.sum(grad_pre, axis=0))
    grad_weight = jnp.dot(hidden.T, grad_pre, precision=lax.Precision.HIGHEST)
    grad_agg = scale_rows * jnp.dot(grad_pre, weight_full.T, precision=lax.Precision.HIGHEST)
    grad_scaled = aggregate(grad_agg, adjacency_tiles, tile_positions, tile_counts, True)
    grad_features = (scale_rows * grad_scaled).astype(jnp.bfloat16)
    return (activations, grad_features, grad_weight, grad_bias)
```

```python
import jax
import jax.numpy as jnp
from jax import lax
from jax.experimental import pallas as pl
from jax.experimental.pallas import tpu as pltpu
from jax.sharding import PartitionSpec as P

MESH = pl.DeviceIdType.MESH
F32 = jnp.float32
BF16 = jnp.bfloat16
I32 = jnp.int32
UNROLL = 8
MAX_COPIES = 192


def two_parts(values):
    upper = values.astype(BF16)
    return upper, (values - upper.astype(F32)).astype(BF16)


def dot(a, b):
    return jnp.dot(a, b, preferred_element_type=F32)


def dot_general(a, b, dims):
    return lax.dot_general(a, b, (dims, ((), ())), preferred_element_type=F32)


def segment_plan(key, shift, eye, lane2, sub2, slots):
    key_col = jnp.sum(jnp.where(eye, key.astype(F32), 0.0), axis=1, keepdims=True).astype(I32)
    less = key < key_col
    rank = jnp.sum(jnp.where(less, 1.0, 0.0), axis=1, keepdims=True).astype(I32)
    seg_col = key_col >> shift
    before = jnp.where(less, 1.0, 0.0) * jnp.where((key >> shift) == seg_col, 1.0, 0.0)
    same = jnp.max(before, axis=1, keepdims=True)
    perm = rank == lane2

    def permuted(column):
        return jnp.sum(jnp.where(perm, column, 0.0), axis=0, keepdims=True).astype(I32)

    order = permuted(sub2.astype(F32))
    sorted_key = permuted(key_col.astype(F32))
    sorted_same = permuted(same)
    upto = jnp.sum(jnp.where(seg_col <= lane2, 1.0, 0.0), axis=0, keepdims=True).astype(I32)
    here = jnp.sum(jnp.where(seg_col == lane2, 1.0, 0.0), axis=0, keepdims=True).astype(I32)
    last = jnp.where(here > 0, upto - 1, slots)
    return order, sorted_key, sorted_same, last


def layer_kernel(
    feat_ref, weight_hbm, bias_ref, cot_hbm, deg_ref, tiles_hbm, pos_ref, cnt_ref,
    act_ref, gf_ref, gw_ref, gb_ref,
    tiles, weight_v, cot_v, table_v, table, gathered, run, part, transit, landed, quarter, own_small,
    transit_q, landed_q, halves, z_send, z_recv, grads, hid_v, pre_v, back, back_in, back_sum, back_recv,
    gw_part, gw_in, gw_x, gw_y, gw_z, gw_all, local_sem, send_sem, recv_sem,
):
    slots, blk, _ = tiles.shape
    row = lax.axis_index("row")
    col = lax.axis_index("col")
    core = lax.rem(row, 2)
    zl = row // 2
    x = col // 8
    zh = lax.rem(col // 4, 2)
    y = lax.rem(col, 4)

    def step4(v, d):
        return lax.rem(v + d, 4)

    def at_x(d):
        return (row, step4(x, d) * 8 + zh * 4 + y)

    def at_y(d):
        return (row, x * 8 + zh * 4 + step4(y, d))

    def at_row(other):
        return (other, col)

    z_peer = (row, x * 8 + (1 - zh) * 4 + y)
    sibling = at_row(zl * 2 + 1 - core)

    barrier = pltpu.get_barrier_semaphore()
    peers = [at_x(d) for d in (1, 2, 3)] + [at_y(d) for d in (1, 2, 3)] + [z_peer]
    peers += [at_row(lax.rem(row + d, 8)) for d in range(1, 8)]
    for peer in peers:
        pl.semaphore_signal(barrier, inc=1, device_id=peer, device_id_type=MESH)

    tiles_copy = pltpu.make_async_copy(tiles_hbm, tiles, local_sem.at[0])
    tiles_copy.start()
    weight_copy = pltpu.make_async_copy(weight_hbm, weight_v, local_sem.at[1])
    weight_copy.start()
    cot_copy = pltpu.make_async_copy(cot_hbm, cot_v, local_sem.at[2])
    cot_copy.start()

    eye_b = lax.broadcasted_iota(I32, (blk, blk), 0) == lax.broadcasted_iota(I32, (blk, blk), 1)
    scale_row = [lax.rsqrt(deg_ref[pl.ds(b, 1), :].astype(F32)) for b in range(2)]
    scale_col = [jnp.sum(jnp.where(eye_b, s, 0.0), axis=1, keepdims=True) for s in scale_row]
    for b in range(2):
        rows = pl.ds(b * blk, blk)
        gathered[row * 2 + b] = (scale_col[b] * feat_ref[rows, :].astype(F32)).astype(BF16)

    pl.semaphore_wait(barrier, len(peers))

    started = []

    def send(src, dst, device):
        n = len(started)
        copy = pltpu.make_async_remote_copy(
            src_ref=src, dst_ref=dst, send_sem=send_sem.at[n], recv_sem=recv_sem.at[n],
            device_id=device, device_id_type=MESH,
        )
        copy.start()
        started.append(copy)
        return copy

    def own_pair(r):
        return gathered.at[pl.ds(r * 2, 2)]

    far = [send(own_pair(row), own_pair(row), at_row(step4(zl, d) * 2 + core)) for d in (1, 2, 3)]
    near = [send(own_pair(row), own_pair(row), sibling)]

    pos = pos_ref[...]
    lane = lax.broadcasted_iota(I32, (1, slots), 1)
    live = lane < cnt_ref[0, 0]
    lane2 = lax.broadcasted_iota(I32, (slots, slots), 1)
    sub2 = lax.broadcasted_iota(I32, (slots, slots), 0)
    eye = lane2 == sub2
    key_f = jnp.where(live, pos, 1024 + lane)
    key_b = jnp.where(live, (pos & 15) * 64 + (pos >> 4), 1024 + lane)
    order_f, sorted_f, same_f, last_f = segment_plan(key_f, 4, eye, lane2, sub2, slots)
    order_b, sorted_b, same_b, last_b = segment_plan(key_b, 6, eye, lane2, sub2, slots)
    rb = sorted_b & 63
    rb_x, rb_z, rb_y = rb >> 4, (rb >> 3) & 1, (rb >> 1) & 3
    slot_b = jnp.where((rb & 1) == 0, (rb_y * 4 + rb_x) * 2 + rb_z, 32 + (rb_x * 4 + rb_y) * 2 + rb_z)
    for n, line in enumerate((order_f, sorted_f & 15, same_f, last_f, order_b, slot_b, same_b, last_b)):
        table_v[pl.ds(n, 1), :] = line
    table_copy = pltpu.make_async_copy(table_v, table, local_sem.at[3])
    table_copy.start()
    run[slots] = jnp.zeros((blk, run.shape[2]), BF16)
    table_copy.wait()
    tiles_copy.wait()

    for d in (1, 2, 3):
        far[d - 1].wait_recv()
        other = step4(zl, 4 - d) * 2 + core
        near.append(send(own_pair(other), own_pair(other), sibling))
    for copy in near:
        copy.wait_recv()

    def forward(g, acc):
        steps = [g * UNROLL + u for u in range(UNROLL)]
        terms = [dot(tiles[table[0, p] & (slots - 1)], gathered[table[1, p] & 15]) for p in steps]
        for p, term in zip(steps, terms):
            acc = acc * table[2, p].astype(F32) + term
            run[p] = acc.astype(BF16)
        return acc

    zero = jnp.zeros((blk, run.shape[2]), F32)
    lax.fori_loop(0, slots // UNROLL, forward, zero)

    def ending(line, segment):
        return jnp.clip(table[line, segment], 0, slots)

    def place(c, carry):
        cx, cz, cy = c // 8, lax.rem(c // 4, 2), lax.rem(c, 4)
        part[0, cy, cx, cz] = run[ending(3, c * 2)]
        part[1, cx, cy, cz] = run[ending(3, c * 2 + 1)]
        return carry

    lax.fori_loop(0, 32, place, 0)

    big, small = (y, x), (x, y)
    at_big, at_small = (at_y, at_x), (at_x, at_y)
    offsets = (2, 1, 3, 0)
    copies = {}

    def issue(h, n):
        q = step4(small[h], offsets[n])
        opp, right, left = (step4(big[h], d) for d in (2, 1, 3))
        up, down = at_big[h](1), at_big[h](3)
        copies[h, n] = [
            send(part.at[h, opp, q, 0], transit.at[h, n, 0], up),
            send(part.at[h, opp, q, 1], transit.at[h, n, 1], down),
            send(part.at[h, right, q, 1], landed.at[h, n, 0, 1], up),
            send(part.at[h, left, q, 0], landed.at[h, n, 1, 0], down),
        ]

    def combine(h, n):
        q = step4(small[h], offsets[n])
        right, left = step4(big[h], 1), step4(big[h], 3)
        c = copies[h, n]
        c[0].wait_recv()
        part[h, right, q, 0] = (part[h, right, q, 0].astype(F32) + transit[h, n, 0].astype(F32)).astype(BF16)
        c.append(send(part.at[h, right, q, 0], landed.at[h, n, 0, 0], at_big[h](1)))
        c[1].wait_recv()
        part[h, left, q, 1] = (part[h, left, q, 1].astype(F32) + transit[h, n, 1].astype(F32)).astype(BF16)
        c.append(send(part.at[h, left, q, 1], landed.at[h, n, 1, 1], at_big[h](3)))

    def finish(h, n):
        q = step4(small[h], offsets[n])
        for c in copies[h, n][2:]:
            c.wait_recv()
        for z in range(2):
            total = (
                part[h, big[h], q, z].astype(F32)
                + landed[h, n, 0, z].astype(F32)
                + landed[h, n, 1, z].astype(F32)
            )
            if n < 3:
                quarter[h, n, z] = total.astype(BF16)
            else:
                own_small[h, z] = total

    def small_first(h):
        copies[h, "s"] = [
            send(quarter.at[h, 0, 0], transit_q.at[h, 0], at_small[h](1)),
            send(quarter.at[h, 0, 1], transit_q.at[h, 1], at_small[h](3)),
        ]

    def small_up(h):
        c = copies[h, "s"]
        c.append(send(quarter.at[h, 1, 1], landed_q.at[h, 0, 1], at_small[h](1)))
        c[0].wait_recv()
        quarter[h, 1, 0] = (quarter[h, 1, 0].astype(F32) + transit_q[h, 0].astype(F32)).astype(BF16)
        c.append(send(quarter.at[h, 1, 0], landed_q.at[h, 0, 0], at_small[h](1)))

    def small_down(h):
        c = copies[h, "s"]
        c.append(send(quarter.at[h, 2, 0], landed_q.at[h, 1, 0], at_small[h](3)))
        c[1].wait_recv()
        quarter[h, 2, 1] = (quarter[h, 2, 1].astype(F32) + transit_q[h, 1].astype(F32)).astype(BF16)
        c.append(send(quarter.at[h, 2, 1], landed_q.at[h, 1, 1], at_small[h](3)))

    def small_finish(h):
        for c in copies[h, "s"][2:]:
            c.wait_recv()
        for z in range(2):
            halves[h, z] = (
                own_small[h, z] + landed_q[h, 0, z].astype(F32) + landed_q[h, 1, z].astype(F32)
            )
        z_send[h] = halves[h, 1 - zh].astype(BF16)
        copies[h, "z"] = send(z_send.at[h], z_recv.at[h], z_peer)

    both = (0, 1)
    for n in (0, 1):
        for h in both:
            issue(h, n)
    for h in both:
        combine(h, 0)
    for h in both:
        issue(h, 2)
    for h in both:
        combine(h, 1)
    for h in both:
        issue(h, 3)
    for h in both:
        finish(h, 0)
        small_first(h)
    for h in both:
        combine(h, 2)
    for h in both:
        finish(h, 1)
        small_up(h)
    for h in both:
        combine(h, 3)
    for h in both:
        finish(h, 2)
        small_down(h)
    for h in both:
        finish(h, 3)
    for h in both:
        small_finish(h)

    weight_copy.wait()
    cot_copy.wait()
    weight = weight_v[...]
    bias = bias_ref[...]
    first, second = zh, 1 - zh

    def spread(h, cs, z, key, both_ways=True):
        ref = grads.at[h, big[h], cs, z]
        copies[h, "b", key] = (send(ref, ref, at_big[h](1)), send(ref, ref, at_big[h](3)))

    def spread_small(h, z, key):
        ref = grads.at[h, big[h], small[h], z]
        copies[h, "p", key] = (send(ref, ref, at_small[h](1)), send(ref, ref, at_small[h](3)))

    for h in both:
        copies[h, "z"].wait_recv()
        hidden = scale_col[h] * (halves[h, zh] + z_recv[h].astype(F32))
        upper, lower = two_parts(hidden)
        preact = dot(upper, weight) + dot(lower, weight) + bias
        gate = 1.0 / (1.0 + jnp.exp(-preact))
        rows = pl.ds(h * blk, blk)
        act_ref[rows, :] = (preact * gate).astype(BF16)
        grad_pre = cot_v[rows, :].astype(F32) * gate * (1.0 + preact * (1.0 - gate))
        hid_v[h] = hidden
        pre_v[h] = grad_pre
        upper, lower = two_parts(grad_pre)
        nt = ((1,), (1,))
        outgoing = scale_row[h] * (dot_general(weight, upper, nt) + dot_general(weight, lower, nt))
        grads[h, big[h], small[h], first] = outgoing.astype(BF16)
        ref = grads.at[h, big[h], small[h], first]
        copies[h, "g"] = send(ref, ref, z_peer)
        spread_small(h, first, "a")
        spread(h, small[h], first, (0, "a"))

    total = None
    bias_sum = None
    tn = ((0,), (0,))
    for h in both:
        hu, hl = two_parts(hid_v[h])
        gu, gl = two_parts(pre_v[h])
        term = dot_general(hu, gu, tn) + dot_general(hu, gl, tn) + dot_general(hl, gu, tn)
        sums = jnp.sum(pre_v[h], axis=0, keepdims=True)
        total = term if total is None else total + term
        bias_sum = sums if bias_sum is None else bias_sum + sums
    share = total.shape[0] // 8
    for r in range(8):
        gw_part[r, pl.ds(0, share), :] = total[r * share:(r + 1) * share, :]
        gw_part[r, pl.ds(share, 8), :] = jnp.broadcast_to(bias_sum, (8, bias_sum.shape[1]))
    gw1 = []
    for d in range(1, 8):
        other = lax.rem(row + d, 8)
        gw1.append(send(gw_part.at[other], gw_in.at[d - 1], at_row(other)))

    for h in both:
        copies[h, "g"].wait_recv()
        spread_small(h, second, "b")
        spread(h, small[h], second, (0, "b"))

    def forward_small(h, key):
        up, down = copies[h, "p", key]
        z = first if key == "a" else second
        left, right = step4(small[h], 3), step4(small[h], 1)
        if key == "a":
            up.wait_recv()
            ref = grads.at[h, big[h], left, z]
            copies[h, "f", key] = send(ref, ref, at_small[h](1))
            spread(h, left, z, (3, key))
            down.wait_recv()
            spread(h, right, z, (1, key))
        else:
            down.wait_recv()
            ref = grads.at[h, big[h], right, z]
            copies[h, "f", key] = send(ref, ref, at_small[h](3))
            spread(h, right, z, (1, key))
            up.wait_recv()
            spread(h, left, z, (3, key))

    def forward_big(h, off, key):
        up, down = copies[h, "b", (off, key)]
        cs = step4(small[h], off)
        if key == "a":
            up.wait_recv()
            ref = grads.at[h, step4(big[h], 3), cs, first]
            copies[h, "w", (off, key)] = send(ref, ref, at_big[h](1))
        else:
            down.wait_recv()
            ref = grads.at[h, step4(big[h], 1), cs, second]
            copies[h, "w", (off, key)] = send(ref, ref, at_big[h](3))

    def finish_big(h, off, key):
        up, down = copies[h, "b", (off, key)]
        (down if key == "a" else up).wait_recv()
        copies[h, "w", (off, key)].wait_recv()

    for key in ("a", "b"):
        for h in both:
            forward_small(h, key)
        for h in both:
            forward_big(h, 0, key)
    for key in ("a", "b"):
        for h in both:
            copies[h, "f", key].wait_recv()
            spread(h, step4(small[h], 2), first if key == "a" else second, (2, key))
        for h in both:
            forward_big(h, 3, key)
            forward_big(h, 1, key)

    for copy in gw1:
        copy.wait_recv()
    piece = gw_part[row]
    for d in range(7):
        piece = piece + gw_in[d]
    gw_x[x] = piece
    gw2 = [send(gw_x.at[x], gw_x.at[x], at_x(d)) for d in (1, 2, 3)]

    for key in ("a", "b"):
        for h in both:
            forward_big(h, 2, key)
    for off in (0, 1, 3, 2):
        for key in ("a", "b"):
            for h in both:
                finish_big(h, off, key)

    for copy in gw2:
        copy.wait_recv()
    gw_y[y] = gw_x[0] + gw_x[1] + gw_x[2] + gw_x[3]
    gw3 = [send(gw_y.at[y], gw_y.at[y], at_y(d)) for d in (1, 2, 3)]

    def backward(g, acc):
        steps = [g * UNROLL + u for u in range(UNROLL)]
        terms = [dot(flat_grad(table[5, p] & 63), tiles[table[4, p] & (slots - 1)]) for p in steps]
        for p, term in zip(steps, terms):
            acc = acc * table[6, p].astype(F32) + term
            run[p] = acc.astype(BF16)
        return acc

    def flat_grad(s):
        return grads[s // 32, lax.rem(s // 8, 4), lax.rem(s // 2, 4), lax.rem(s, 2)]

    zero_t = jnp.zeros((run.shape[1], blk), F32)
    mid = slots // UNROLL // 2
    acc = lax.fori_loop(0, mid, backward, zero_t)
    for copy in gw3:
        copy.wait_recv()
    gw_z[zh] = gw_y[0] + gw_y[1] + gw_y[2] + gw_y[3]
    gw4 = send(gw_z.at[zh], gw_z.at[zh], z_peer)
    lax.fori_loop(mid, slots // UNROLL, backward, acc)

    def place_back(r, carry):
        for b in range(2):
            back[lax.rem(r, 2), r // 2, b] = run[ending(7, r * 2 + b)]
        return carry

    lax.fori_loop(0, 8, place_back, 0)

    near = []
    for d in (1, 2, 3, 0):
        other = step4(zl, d)
        near.append(send(back.at[1 - core, other], back_in.at[d], sibling))
    gw4.wait_recv()
    gw_all[row] = gw_z[0] + gw_z[1]
    gw5 = [send(gw_all.at[row], gw_all.at[row], at_row(lax.rem(row + d, 8))) for d in range(1, 8)]
    far = []
    for n, d in enumerate((1, 2, 3)):
        other = step4(zl, d)
        near[n].wait_recv()
        back_sum[n] = (back[core, other].astype(F32) + back_in[d].astype(F32)).astype(BF16)
        far.append(send(back_sum.at[n], back_recv.at[n], at_row(other * 2 + core)))
    near[3].wait_recv()
    own = back[core, zl].astype(F32) + back_in[0].astype(F32)
    for copy in gw5:
        copy.wait_recv()
    for r in range(8):
        gw_ref[pl.ds(r * share, share), :] = gw_all[r, pl.ds(0, share), :]
    gb_ref[...] = gw_all[0, pl.ds(share, 1), :]
    for n in range(3):
        far[n].wait_recv()
        own = own + back_recv[n].astype(F32)
    for b in range(2):
        gf_ref[pl.ds(b * blk, blk), :] = jnp.transpose(scale_row[b] * own[b]).astype(BF16)

    assert len(started) <= MAX_COPIES
    for copy in started:
        copy.wait_send()


def per_device(
    features, weight, bias_vector, cotangent, degrees, adjacency_tiles, tile_positions, tile_counts
):
    slots, blk = adjacency_tiles.shape[2:4]
    f_in, hid = weight.shape
    nodes = features.shape[0]
    share = f_in // 8
    vmem = pl.BlockSpec(memory_space=pltpu.VMEM)
    anywhere = pl.BlockSpec(memory_space=pl.ANY)
    piece = (share + 8, hid)
    outs = pl.pallas_call(
        layer_kernel,
        out_shape=(
            jax.ShapeDtypeStruct((nodes, hid), BF16),
            jax.ShapeDtypeStruct((nodes, f_in), BF16),
            jax.ShapeDtypeStruct((f_in, hid), F32),
            jax.ShapeDtypeStruct((1, hid), F32),
        ),
        in_specs=[
            vmem, anywhere, vmem, anywhere, vmem, anywhere, vmem, pl.BlockSpec(memory_space=pltpu.SMEM),
        ],
        out_specs=(vmem, vmem, vmem, vmem),
        scratch_shapes=[
            pltpu.VMEM((slots, blk, blk), BF16),
            pltpu.VMEM((f_in, hid), BF16),
            pltpu.VMEM((nodes, hid), BF16),
            pltpu.VMEM((8, slots), I32),
            pltpu.SMEM((8, slots), I32),
            pltpu.VMEM((16, blk, f_in), BF16),
            pltpu.VMEM((slots + 1, blk, f_in), BF16),
            pltpu.VMEM((2, 4, 4, 2, blk, f_in), BF16),
            pltpu.VMEM((2, 4, 2, blk, f_in), BF16),
            pltpu.VMEM((2, 4, 2, 2, blk, f_in), BF16),
            pltpu.VMEM((2, 3, 2, blk, f_in), BF16),
            pltpu.VMEM((2, 2, blk, f_in), F32),
            pltpu.VMEM((2, 2, blk, f_in), BF16),
            pltpu.VMEM((2, 2, 2, blk, f_in), BF16),
            pltpu.VMEM((2, 2, blk, f_in), F32),
            pltpu.VMEM((2, blk, f_in), BF16),
            pltpu.VMEM((2, blk, f_in), BF16),
            pltpu.VMEM((2, 4, 4, 2, f_in, blk), BF16),
            pltpu.VMEM((2, blk, f_in), F32),
            pltpu.VMEM((2, blk, hid), F32),
            pltpu.VMEM((2, 4, 2, f_in, blk), BF16),
            pltpu.VMEM((4, 2, f_in, blk), BF16),
            pltpu.VMEM((3, 2, f_in, blk), BF16),
            pltpu.VMEM((3, 2, f_in, blk), BF16),
            pltpu.VMEM((8,) + piece, F32),
            pltpu.VMEM((7,) + piece, F32),
            pltpu.VMEM((4,) + piece, F32),
            pltpu.VMEM((4,) + piece, F32),
            pltpu.VMEM((2,) + piece, F32),
            pltpu.VMEM((8,) + piece, F32),
            pltpu.SemaphoreType.DMA((4,)),
            pltpu.SemaphoreType.DMA((MAX_COPIES,)),
            pltpu.SemaphoreType.DMA((MAX_COPIES,)),
        ],
        compiler_params=pltpu.CompilerParams(
            collective_id=0, has_side_effects=True, vmem_limit_bytes=40 * 1024 * 1024
        ),
        name="graph_layer",
    )(
        features,
        weight,
        bias_vector.reshape(1, hid),
        cotangent,
        degrees.reshape(2, blk),
        adjacency_tiles.reshape(slots, blk, blk),
        tile_positions.reshape(1, slots),
        tile_counts,
    )
    activations, grad_features, grad_weight, grad_bias = outs
    return activations, grad_features, grad_weight, grad_bias.reshape(hid)


def solution(mesh):
    placed = (
        P(("row", "col"), None),
        P(),
        P(),
        P(("row", "col"), None),
        P(("row", "col")),
        P("row", "col", None, None, None),
        P("row", "col", None),
        P("row", "col"),
    )
    return jax.shard_map(
        per_device,
        mesh=mesh,
        in_specs=placed,
        out_specs=(P(("row", "col"), None), P(("row", "col"), None), P(), P()),
        check_vma=False,
    )
```

```python
import jax
import jax.numpy as jnp
from jax import lax
from jax.experimental import pallas as pl
from jax.experimental.pallas import tpu as pltpu
from jax.sharding import PartitionSpec as P

MESH = pl.DeviceIdType.MESH
F32 = jnp.float32
BF16 = jnp.bfloat16
I32 = jnp.int32
UNROLL = 32
MAX_COPIES = 192
OFFSETS = (2, 1, 3, 0)
VMEM_BYTES = 60 * 1024 * 1024


def two_parts(values):
    upper = values.astype(BF16)
    return upper, (values - upper.astype(F32)).astype(BF16)


def dot(a, b):
    return jnp.dot(a, b, preferred_element_type=F32)


def dot_general(a, b, dims):
    return lax.dot_general(a, b, (dims, ((), ())), preferred_element_type=F32)


def segment_plan(key, shift, eye, lane2, sub2, slots):
    key_col = jnp.sum(jnp.where(eye, key.astype(F32), 0.0), axis=1, keepdims=True).astype(I32)
    less = key < key_col
    rank = jnp.sum(jnp.where(less, 1.0, 0.0), axis=1, keepdims=True).astype(I32)
    seg_col = key_col >> shift
    before = jnp.where(less, 1.0, 0.0) * jnp.where((key >> shift) == seg_col, 1.0, 0.0)
    same = jnp.max(before, axis=1, keepdims=True)
    perm = rank == lane2

    def permuted(column):
        return jnp.sum(jnp.where(perm, column, 0.0), axis=0, keepdims=True).astype(I32)

    order = permuted(sub2.astype(F32))
    sorted_key = permuted(key_col.astype(F32))
    sorted_same = permuted(same)
    upto = jnp.sum(jnp.where(seg_col <= lane2, 1.0, 0.0), axis=0, keepdims=True).astype(I32)
    here = jnp.sum(jnp.where(seg_col == lane2, 1.0, 0.0), axis=0, keepdims=True).astype(I32)
    last = jnp.where(here > 0, upto - 1, slots)
    return order, sorted_key, sorted_same, last


def layer_kernel(
    feat_hbm, weight_hbm, bias_hbm, cot_hbm, deg_hbm, tiles_hbm, pos_hbm, cnt_hbm,
    act_hbm, gf_hbm, gw_hbm, gb_hbm,
    feat_ref, bias_ref, deg_ref, pos_ref, cnt_ref, act_ref, gf_ref, gw_ref, gb_ref,
    tiles, weight_v, cot_v, table_v, table, gathered, run, part, landed, quarter, own_small,
    landed_q, halves, z_send, z_recv, grads, hid_v, pre_v, back, back_in, back_sum, back_recv,
    gw_part, gw_in, gw_sum, gw_row, gw_x, gw_y, gw_z, gw_all, local_sem, send_sem, recv_sem,
):
    slots, blk, _ = tiles.shape
    row = lax.axis_index("row")
    col = lax.axis_index("col")
    core = lax.rem(row, 2)
    zl = row // 2
    x = col // 8
    zh = lax.rem(col // 4, 2)
    y = lax.rem(col, 4)

    def step4(v, d):
        return lax.rem(v + d, 4)

    def at_x(d):
        return (row, step4(x, d) * 8 + zh * 4 + y)

    def at_y(d):
        return (row, x * 8 + zh * 4 + step4(y, d))

    def at_row(other):
        return (other, col)

    z_peer = (row, x * 8 + (1 - zh) * 4 + y)
    sibling = at_row(zl * 2 + 1 - core)

    barrier = pltpu.get_barrier_semaphore()
    peers = [at_x(d) for d in (1, 2, 3)] + [at_y(d) for d in (1, 2, 3)] + [z_peer]
    peers += [at_row(lax.rem(row + d, 8)) for d in range(1, 8)]
    for peer in peers:
        pl.semaphore_signal(barrier, inc=1, device_id=peer, device_id_type=MESH)

    def bring(n, src, dst):
        copy = pltpu.make_async_copy(src, dst, local_sem.at[n])
        copy.start()
        return copy

    pos_copy = bring(0, pos_hbm, pos_ref)
    cnt_copy = bring(8, cnt_hbm, cnt_ref)
    deg_copy = bring(1, deg_hbm, deg_ref)
    feat_copy = bring(2, feat_hbm, feat_ref)
    tiles_copy = bring(3, tiles_hbm, tiles)
    weight_copy = bring(4, weight_hbm, weight_v)
    cot_copy = bring(5, cot_hbm, cot_v)
    bias_copy = bring(6, bias_hbm, bias_ref)

    pos_copy.wait()
    cnt_copy.wait()
    pos = pos_ref[...]
    lane = lax.broadcasted_iota(I32, (1, slots), 1)
    live = lane < cnt_ref[...]
    lane2 = lax.broadcasted_iota(I32, (slots, slots), 1)
    sub2 = lax.broadcasted_iota(I32, (slots, slots), 0)
    eye = lane2 == sub2
    key_f = jnp.where(live, pos, 1024 + lane)
    key_b = jnp.where(live, (pos & 15) * 64 + (pos >> 4), 1024 + lane)
    order_f, sorted_f, same_f, last_f = segment_plan(key_f, 4, eye, lane2, sub2, slots)
    order_b, sorted_b, same_b, last_b = segment_plan(key_b, 6, eye, lane2, sub2, slots)
    rb = sorted_b & 63
    rb_x, rb_z, rb_y = rb >> 4, (rb >> 3) & 1, (rb >> 1) & 3
    slot_b = jnp.where((rb & 1) == 0, (rb_y * 4 + rb_x) * 2 + rb_z, 32 + (rb_x * 4 + rb_y) * 2 + rb_z)
    for n, line in enumerate((order_f, sorted_f & 15, same_f, last_f, order_b, slot_b, same_b, last_b)):
        table_v[pl.ds(n, 1), :] = line
    table_copy = bring(7, table_v, table)
    run[slots] = jnp.zeros((blk, run.shape[2]), BF16)

    deg_copy.wait()
    feat_copy.wait()
    eye_b = lax.broadcasted_iota(I32, (blk, blk), 0) == lax.broadcasted_iota(I32, (blk, blk), 1)
    scale_row = [lax.rsqrt(deg_ref[pl.ds(b, 1), :].astype(F32)) for b in range(2)]
    scale_col = [jnp.sum(jnp.where(eye_b, s, 0.0), axis=1, keepdims=True) for s in scale_row]
    for b in range(2):
        rows = pl.ds(b * blk, blk)
        gathered[row * 2 + b] = (scale_col[b] * feat_ref[rows, :].astype(F32)).astype(BF16)

    pl.semaphore_wait(barrier, len(peers))

    started = []

    def send(src, dst, device):
        n = len(started)
        copy = pltpu.make_async_remote_copy(
            src_ref=src, dst_ref=dst, send_sem=send_sem.at[n], recv_sem=recv_sem.at[n],
            device_id=device, device_id_type=MESH,
        )
        copy.start()
        started.append(copy)
        return copy

    def own_pair(r):
        return gathered.at[pl.ds(r * 2, 2)]

    far = [send(own_pair(row), own_pair(row), at_row(step4(zl, d) * 2 + core)) for d in (1, 2, 3)]
    near = [send(own_pair(row), own_pair(row), sibling)]

    for d in (1, 2, 3):
        far[d - 1].wait_recv()
        other = step4(zl, 4 - d) * 2 + core
        near.append(send(own_pair(other), own_pair(other), sibling))
    for copy in near:
        copy.wait_recv()

    table_copy.wait()
    tiles_copy.wait()

    def forward(g, acc):
        steps = [g * UNROLL + u for u in range(UNROLL)]
        terms = [dot(tiles[table[0, p] & (slots - 1)], gathered[table[1, p] & 15]) for p in steps]
        for p, term in zip(steps, terms):
            acc = acc * table[2, p].astype(F32) + term
            run[p] = acc.astype(BF16)
        return acc

    zero = jnp.zeros((blk, run.shape[2]), F32)
    lax.fori_loop(0, slots // UNROLL, forward, zero)

    def ending(line, segment):
        return jnp.clip(table[line, segment], 0, slots)

    def place(c, carry):
        cx, cz, cy = c // 8, lax.rem(c // 4, 2), lax.rem(c, 4)
        part[0, cy, cx, cz] = run[ending(3, c * 2)]
        part[1, cx, cy, cz] = run[ending(3, c * 2 + 1)]
        return carry

    lax.fori_loop(0, 32, place, 0)

    big, small = (y, x), (x, y)
    at_big, at_small = (at_y, at_x), (at_x, at_y)
    layers = (1 - zh, zh)
    both = (0, 1)
    copies = {}

    def issue(n, lay):
        for h in both:
            q = step4(small[h], OFFSETS[n])
            copies[h, lay, n] = [
                send(part.at[h, step4(big[h], d), q, layers[lay]], landed.at[h, lay, n, d - 1], at_big[h](d))
                for d in (2, 1, 3)
            ]

    def finish(n, lay):
        for h in both:
            q = step4(small[h], OFFSETS[n])
            total = part[h, big[h], q, layers[lay]].astype(F32)
            for d, c in zip((2, 1, 3), copies[h, lay, n]):
                c.wait_recv()
                total = total + landed[h, lay, n, d - 1].astype(F32)
            if n < 3:
                quarter[h, lay, n] = total.astype(BF16)
                copies[h, lay, "s", n] = send(
                    quarter.at[h, lay, n], landed_q.at[h, lay, n], at_small[h](OFFSETS[n])
                )
            else:
                own_small[h, lay] = total

    def small_finish(lay):
        for h in both:
            total = own_small[h, lay]
            for n in range(3):
                copies[h, lay, "s", n].wait_recv()
                total = total + landed_q[h, lay, n].astype(F32)
            if lay == 0:
                z_send[h] = total.astype(BF16)
                copies[h, "z"] = send(z_send.at[h], z_recv.at[h], z_peer)
            else:
                halves[h] = total

    for n in range(4):
        issue(n, 0)
    for n in range(4):
        finish(n, 0)
        issue(n, 1)
    small_finish(0)
    for n in range(4):
        finish(n, 1)
    small_finish(1)

    weight_copy.wait()
    cot_copy.wait()
    bias_copy.wait()
    weight = weight_v[...]
    bias = bias_ref[...]

    def spread(h, off, lay):
        ref = grads.at[h, big[h], step4(small[h], off), layers[lay]]
        copies[h, "b", off, lay] = [send(ref, ref, at_big[h](d)) for d in (2, 1, 3)]

    def spread_small(h, lay):
        ref = grads.at[h, big[h], small[h], layers[lay]]
        copies[h, "p", lay] = [send(ref, ref, at_small[h](d)) for d in (2, 1, 3)]

    def pass_on(lay):
        for d, n in ((1, 1), (3, 2), (2, 0)):
            for h in both:
                copies[h, "p", lay][n].wait_recv()
                spread(h, 4 - d, lay)

    for h in both:
        copies[h, "z"].wait_recv()
        hidden = scale_col[h] * (halves[h] + z_recv[h].astype(F32))
        upper, lower = two_parts(hidden)
        preact = dot(upper, weight) + dot(lower, weight) + bias
        gate = 1.0 / (1.0 + jnp.exp(-preact))
        rows = pl.ds(h * blk, blk)
        act_ref[rows, :] = (preact * gate).astype(BF16)
        grad_pre = cot_v[rows, :].astype(F32) * gate * (1.0 + preact * (1.0 - gate))
        hid_v[h] = hidden
        pre_v[h] = grad_pre
        upper, lower = two_parts(grad_pre)
        nt = ((1,), (1,))
        outgoing = scale_row[h] * (dot_general(weight, upper, nt) + dot_general(weight, lower, nt))
        grads[h, big[h], small[h], zh] = outgoing.astype(BF16)
        ref = grads.at[h, big[h], small[h], zh]
        copies[h, "g"] = send(ref, ref, z_peer)
        spread_small(h, 1)
        spread(h, 0, 1)

    out_copies = [bring(0, act_ref, act_hbm)]

    total = None
    bias_sum = None
    tn = ((0,), (0,))
    for h in both:
        hu, hl = two_parts(hid_v[h])
        gu, gl = two_parts(pre_v[h])
        term = dot_general(hu, gu, tn) + dot_general(hu, gl, tn) + dot_general(hl, gu, tn)
        sums = jnp.sum(pre_v[h], axis=0, keepdims=True)
        total = term if total is None else total + term
        bias_sum = sums if bias_sum is None else bias_sum + sums
    share = total.shape[0] // 8
    for r in range(8):
        gw_part[r % 2, r // 2, pl.ds(0, share), :] = total[r * share:(r + 1) * share, :]
        gw_part[r % 2, r // 2, pl.ds(share, 8), :] = jnp.broadcast_to(bias_sum, (8, bias_sum.shape[1]))
    gw_near = send(gw_part.at[1 - core], gw_in, sibling)

    pass_on(1)
    gw_near.wait_recv()
    for z in range(4):
        gw_sum[z] = gw_part[core, z] + gw_in[z]
    gw_row[zl] = gw_sum[zl]
    gw_far = []
    for d in (1, 2, 3):
        other = step4(zl, d)
        gw_far.append(send(gw_sum.at[other], gw_row.at[zl], at_row(other * 2 + core)))
    for h in both:
        copies[h, "g"].wait_recv()
        spread_small(h, 0)
        spread(h, 0, 0)
    pass_on(0)

    for copy in gw_far:
        copy.wait_recv()
    gw_z[zh] = gw_row[0] + gw_row[1] + gw_row[2] + gw_row[3]
    gw_across = send(gw_z.at[zh], gw_z.at[zh], z_peer)

    def arrive(lay):
        for off in (0, 1, 3, 2):
            for h in both:
                for copy in copies[h, "b", off, lay]:
                    copy.wait_recv()

    arrive(1)
    gw_across.wait_recv()
    gw_x[x] = gw_z[0] + gw_z[1]
    gw_along_x = [send(gw_x.at[x], gw_x.at[x], at_x(d)) for d in (1, 2, 3)]
    arrive(0)

    def backward(g, acc):
        steps = [g * UNROLL + u for u in range(UNROLL)]
        terms = [dot(flat_grad(table[5, p] & 63), tiles[table[4, p] & (slots - 1)]) for p in steps]
        for p, term in zip(steps, terms):
            acc = acc * table[6, p].astype(F32) + term
            run[p] = acc.astype(BF16)
        return acc

    def flat_grad(s):
        return grads[s // 32, lax.rem(s // 8, 4), lax.rem(s // 2, 4), lax.rem(s, 2)]

    zero_t = jnp.zeros((run.shape[1], blk), F32)
    lax.fori_loop(0, slots // UNROLL, backward, zero_t)

    def place_back(r, carry):
        for b in range(2):
            back[lax.rem(r, 2), r // 2, b] = run[ending(7, r * 2 + b)]
        return carry

    lax.fori_loop(0, 8, place_back, 0)

    near = []
    for d in (1, 2, 3, 0):
        other = step4(zl, d)
        near.append(send(back.at[1 - core, other], back_in.at[d], sibling))
    far = []
    for n, d in enumerate((1, 2, 3)):
        other = step4(zl, d)
        near[n].wait_recv()
        back_sum[n] = (back[core, other].astype(F32) + back_in[d].astype(F32)).astype(BF16)
        far.append(send(back_sum.at[n], back_recv.at[n], at_row(other * 2 + core)))
    for copy in gw_along_x:
        copy.wait_recv()
    gw_y[y] = gw_x[0] + gw_x[1] + gw_x[2] + gw_x[3]
    gw_along_y = [send(gw_y.at[y], gw_y.at[y], at_y(d)) for d in (1, 2, 3)]
    near[3].wait_recv()
    own = back[core, zl].astype(F32) + back_in[0].astype(F32)
    for copy in gw_along_y:
        copy.wait_recv()
    piece = gw_y[0] + gw_y[1] + gw_y[2] + gw_y[3]
    gb_ref[...] = piece[share:share + 1, :]
    gw_all[row] = piece[:share, :].astype(BF16)
    mine = gw_all.at[row]
    gw_out = [send(mine, mine, at_row(lax.rem(row + d, 8))) for d in range(1, 8)]
    for copy in gw_out:
        copy.wait_recv()
    for r in range(8):
        gw_ref[pl.ds(r * share, share), :] = gw_all[r].astype(F32)
    out_copies += [bring(1, gw_ref, gw_hbm), bring(2, gb_ref, gb_hbm)]
    for n in range(3):
        far[n].wait_recv()
        own = own + back_recv[n].astype(F32)
    for b in range(2):
        gf_ref[pl.ds(b * blk, blk), :] = jnp.transpose(scale_row[b] * own[b]).astype(BF16)

    out_copies.append(bring(3, gf_ref, gf_hbm))
    assert len(started) <= MAX_COPIES
    for copy in out_copies:
        copy.wait()
    for copy in started:
        copy.wait_send()


def deliver_kernel(*refs):
    ins, outs, held, sems = refs[:4], refs[4:8], refs[8:12], refs[12]
    moves = [pltpu.make_async_copy(ins[n], held[n], sems.at[n]) for n in range(4)]
    moves += [pltpu.make_async_copy(held[n], outs[n], sems.at[n + 4]) for n in range(4)]
    for move in moves[:4]:
        move.start()
    for n in range(4):
        moves[n].wait()
        moves[n + 4].start()
    for move in moves[4:]:
        move.wait()


def per_device(
    features, weight, bias_vector, cotangent, degrees, adjacency_tiles, tile_positions, tile_counts
):
    slots, blk = adjacency_tiles.shape[2:4]
    f_in, hid = weight.shape
    nodes = features.shape[0]
    share = f_in // 8
    anywhere = pl.BlockSpec(memory_space=pl.ANY)
    piece = (share + 8, hid)
    outs = pl.pallas_call(
        layer_kernel,
        out_shape=(
            jax.ShapeDtypeStruct((nodes, hid), BF16),
            jax.ShapeDtypeStruct((nodes, f_in), BF16),
            jax.ShapeDtypeStruct((f_in, hid), F32),
            jax.ShapeDtypeStruct((1, hid), F32),
        ),
        in_specs=[anywhere] * 8,
        out_specs=(anywhere,) * 4,
        scratch_shapes=[
            pltpu.VMEM((nodes, f_in), BF16),
            pltpu.VMEM((1, hid), F32),
            pltpu.VMEM((2, blk), I32),
            pltpu.VMEM((1, slots), I32),
            pltpu.VMEM((1, 1), I32),
            pltpu.VMEM((nodes, hid), BF16),
            pltpu.VMEM((nodes, f_in), BF16),
            pltpu.VMEM((f_in, hid), F32),
            pltpu.VMEM((1, hid), F32),
            pltpu.VMEM((slots, blk, blk), BF16),
            pltpu.VMEM((f_in, hid), BF16),
            pltpu.VMEM((nodes, hid), BF16),
            pltpu.VMEM((8, slots), I32),
            pltpu.SMEM((8, slots), I32),
            pltpu.VMEM((16, blk, f_in), BF16),
            pltpu.VMEM((slots + 1, blk, f_in), BF16),
            pltpu.VMEM((2, 4, 4, 2, blk, f_in), BF16),
            pltpu.VMEM((2, 2, 4, 3, blk, f_in), BF16),
            pltpu.VMEM((2, 2, 3, blk, f_in), BF16),
            pltpu.VMEM((2, 2, blk, f_in), F32),
            pltpu.VMEM((2, 2, 3, blk, f_in), BF16),
            pltpu.VMEM((2, blk, f_in), F32),
            pltpu.VMEM((2, blk, f_in), BF16),
            pltpu.VMEM((2, blk, f_in), BF16),
            pltpu.VMEM((2, 4, 4, 2, f_in, blk), BF16),
            pltpu.VMEM((2, blk, f_in), F32),
            pltpu.VMEM((2, blk, hid), F32),
            pltpu.VMEM((2, 4, 2, f_in, blk), BF16),
            pltpu.VMEM((4, 2, f_in, blk), BF16),
            pltpu.VMEM((3, 2, f_in, blk), BF16),
            pltpu.VMEM((3, 2, f_in, blk), BF16),
            pltpu.VMEM((2, 4) + piece, F32),
            pltpu.VMEM((4,) + piece, F32),
            pltpu.VMEM((4,) + piece, F32),
            pltpu.VMEM((4,) + piece, F32),
            pltpu.VMEM((4,) + piece, F32),
            pltpu.VMEM((4,) + piece, F32),
            pltpu.VMEM((2,) + piece, F32),
            pltpu.VMEM((8, share, hid), BF16),
            pltpu.SemaphoreType.DMA((9,)),
            pltpu.SemaphoreType.DMA((MAX_COPIES,)),
            pltpu.SemaphoreType.DMA((MAX_COPIES,)),
        ],
        compiler_params=pltpu.CompilerParams(
            collective_id=0, has_side_effects=True, vmem_limit_bytes=VMEM_BYTES
        ),
        name="graph_layer",
    )(
        features,
        weight,
        bias_vector.reshape(1, hid),
        cotangent,
        degrees.reshape(2, blk),
        adjacency_tiles.reshape(slots, blk, blk),
        tile_positions.reshape(1, slots),
        tile_counts,
    )
    activations, grad_features, grad_weight, grad_bias = pl.pallas_call(
        deliver_kernel,
        out_shape=tuple(jax.ShapeDtypeStruct(o.shape, o.dtype) for o in outs),
        in_specs=[anywhere] * 4,
        out_specs=(anywhere,) * 4,
        scratch_shapes=[pltpu.VMEM(o.shape, o.dtype) for o in outs] + [pltpu.SemaphoreType.DMA((8,))],
        compiler_params=pltpu.CompilerParams(vmem_limit_bytes=VMEM_BYTES),
        name="deliver",
    )(*outs)
    return activations, grad_features, grad_weight, grad_bias.reshape(hid)


def solution(mesh):
    placed = (
        P(("row", "col"), None),
        P(),
        P(),
        P(("row", "col"), None),
        P(("row", "col")),
        P("row", "col", None, None, None),
        P("row", "col", None),
        P("row", "col"),
    )
    return jax.shard_map(
        per_device,
        mesh=mesh,
        in_specs=placed,
        out_specs=(P(("row", "col"), None), P(("row", "col"), None), P(), P()),
        check_vma=False,
    )
```

```python
import jax
import jax.numpy as jnp
from jax import lax
from jax.experimental import pallas as pl
from jax.experimental.pallas import tpu as pltpu
from jax.sharding import PartitionSpec as P

MESH = pl.DeviceIdType.MESH
F32 = jnp.float32
BF16 = jnp.bfloat16
I32 = jnp.int32
UNROLL = 32
ARRIVALS = 53
LOTS = 11
OFFSETS = (2, 1, 3, 0)
VMEM_BYTES = 40 * 1024 * 1024


def two_parts(values):
    upper = values.astype(BF16)
    return upper, (values - upper.astype(F32)).astype(BF16)


def dot(a, b):
    return jnp.dot(a, b, preferred_element_type=F32)


def dot_general(a, b, dims):
    return lax.dot_general(a, b, (dims, ((), ())), preferred_element_type=F32)


def segment_plan(key, shift, eye, lane2, sub2, slots):
    key_col = jnp.sum(jnp.where(eye, key.astype(F32), 0.0), axis=1, keepdims=True).astype(I32)
    less = key < key_col
    rank = jnp.sum(jnp.where(less, 1.0, 0.0), axis=1, keepdims=True).astype(I32)
    seg_col = key_col >> shift
    before = jnp.where(less, 1.0, 0.0) * jnp.where((key >> shift) == seg_col, 1.0, 0.0)
    same = jnp.max(before, axis=1, keepdims=True)
    perm = rank == lane2

    def permuted(column):
        return jnp.sum(jnp.where(perm, column, 0.0), axis=0, keepdims=True).astype(I32)

    order = permuted(sub2.astype(F32))
    sorted_key = permuted(key_col.astype(F32))
    sorted_same = permuted(same)
    upto = jnp.sum(jnp.where(seg_col <= lane2, 1.0, 0.0), axis=0, keepdims=True).astype(I32)
    here = jnp.sum(jnp.where(seg_col == lane2, 1.0, 0.0), axis=0, keepdims=True).astype(I32)
    last = jnp.where(here > 0, upto - 1, slots)
    return order, sorted_key, sorted_same, last


def layer_kernel(
    feat_hbm, weight_hbm, bias_hbm, cot_hbm, deg_hbm, tiles_hbm, pos_hbm, cnt_hbm,
    act_ref, gf_ref, gw_ref, gb_ref,
    feat_ref, bias_ref, deg_ref, pos_ref, cnt_ref,
    tiles, weight_v, cot_v, table_v, table, gathered, run, part, landed, quarter, own_small,
    landed_q, halves, z_send, z_recv, grads, hid_v, pre_v, back, back_in, back_sum, back_recv,
    gw_part, gw_in, gw_sum, gw_row, gw_x, gw_y, gw_z, gw_all, gw_wait, local_sem, send_sem, recv_sem,
):
    slots, blk, _ = tiles.shape
    row = lax.axis_index("row")
    col = lax.axis_index("col")
    core = lax.rem(row, 2)
    zl = row // 2
    x = col // 8
    zh = lax.rem(col // 4, 2)
    y = lax.rem(col, 4)

    def step4(v, d):
        return lax.rem(v + d, 4)

    def at_x(d):
        return (row, step4(x, d) * 8 + zh * 4 + y)

    def at_y(d):
        return (row, x * 8 + zh * 4 + step4(y, d))

    def at_row(other):
        return (other, col)

    z_peer = (row, x * 8 + (1 - zh) * 4 + y)
    sibling = at_row(zl * 2 + 1 - core)

    barrier = pltpu.get_barrier_semaphore()
    peers = [at_x(d) for d in (1, 2, 3)] + [at_y(d) for d in (1, 2, 3)] + [z_peer]
    peers += [at_row(lax.rem(row + d, 8)) for d in range(1, 8)]
    for peer in peers:
        pl.semaphore_signal(barrier, inc=1, device_id=peer, device_id_type=MESH)

    def bring(n, src, dst):
        copy = pltpu.make_async_copy(src, dst, local_sem.at[n])
        copy.start()
        return copy

    pos_copy = bring(0, pos_hbm, pos_ref)
    cnt_copy = bring(8, cnt_hbm, cnt_ref)
    deg_copy = bring(1, deg_hbm, deg_ref)
    feat_copy = bring(2, feat_hbm, feat_ref)
    tiles_copy = bring(3, tiles_hbm, tiles)
    weight_copy = bring(4, weight_hbm, weight_v)
    cot_copy = bring(5, cot_hbm, cot_v)
    bias_copy = bring(6, bias_hbm, bias_ref)

    pos_copy.wait()
    cnt_copy.wait()
    pos = pos_ref[...]
    lane = lax.broadcasted_iota(I32, (1, slots), 1)
    live = lane < cnt_ref[...]
    lane2 = lax.broadcasted_iota(I32, (slots, slots), 1)
    sub2 = lax.broadcasted_iota(I32, (slots, slots), 0)
    eye = lane2 == sub2
    key_f = jnp.where(live, pos, 1024 + lane)
    key_b = jnp.where(live, (pos & 15) * 64 + (pos >> 4), 1024 + lane)
    order_f, sorted_f, same_f, last_f = segment_plan(key_f, 4, eye, lane2, sub2, slots)
    order_b, sorted_b, same_b, last_b = segment_plan(key_b, 6, eye, lane2, sub2, slots)
    rb = sorted_b & 63
    rb_x, rb_z, rb_y = rb >> 4, (rb >> 3) & 1, (rb >> 1) & 3
    slot_b = jnp.where((rb & 1) == 0, (rb_y * 4 + rb_x) * 2 + rb_z, 32 + (rb_x * 4 + rb_y) * 2 + rb_z)
    for n, line in enumerate((order_f, sorted_f & 15, same_f, last_f, order_b, slot_b, same_b, last_b)):
        table_v[pl.ds(n, 1), :] = line
    table_copy = bring(7, table_v, table)
    run[slots] = jnp.zeros((blk, run.shape[2]), BF16)

    deg_copy.wait()
    feat_copy.wait()
    eye_b = lax.broadcasted_iota(I32, (blk, blk), 0) == lax.broadcasted_iota(I32, (blk, blk), 1)
    scale_row = [lax.rsqrt(deg_ref[pl.ds(b, 1), :].astype(F32)) for b in range(2)]
    scale_col = [jnp.sum(jnp.where(eye_b, s, 0.0), axis=1, keepdims=True) for s in scale_row]
    for b in range(2):
        rows = pl.ds(b * blk, blk)
        gathered[row * 2 + b] = (scale_col[b] * feat_ref[rows, :].astype(F32)).astype(BF16)

    pl.semaphore_wait(barrier, len(peers))

    slot_of, lots = {}, {}

    def arrival(key):
        return recv_sem.at[slot_of.setdefault(key, len(slot_of))]

    def send(src, dst, device, key, lot):
        copy = pltpu.make_async_remote_copy(
            src_ref=src, dst_ref=dst, send_sem=send_sem.at[lot], recv_sem=arrival(key),
            device_id=device, device_id_type=MESH,
        )
        copy.start()
        lots[lot] = lots.get(lot, 0) + 1
        return copy

    def wait_all(ref, sem):
        pltpu.make_async_copy(ref, ref, sem).wait()

    def own_pair(r):
        return gathered.at[pl.ds(r * 2, 2)]

    mine = own_pair(row)
    far = [send(mine, mine, at_row(step4(zl, d) * 2 + core), ("feat", d), 0) for d in (1, 2, 3)]
    send(mine, mine, sibling, "feat", 0)

    for d in (1, 2, 3):
        far[d - 1].wait_recv()
        other = step4(zl, 4 - d) * 2 + core
        send(own_pair(other), own_pair(other), sibling, "feat", 0)
    wait_all(gathered.at[pl.ds(0, 8)], arrival("feat"))

    table_copy.wait()
    tiles_copy.wait()

    def forward(g, acc):
        steps = [g * UNROLL + u for u in range(UNROLL)]
        terms = [dot(tiles[table[0, p] & (slots - 1)], gathered[table[1, p] & 15]) for p in steps]
        for p, term in zip(steps, terms):
            acc = acc * table[2, p].astype(F32) + term
            run[p] = acc.astype(BF16)
        return acc

    zero = jnp.zeros((blk, run.shape[2]), F32)
    lax.fori_loop(0, slots // UNROLL, forward, zero)

    def ending(line, segment):
        return jnp.clip(table[line, segment], 0, slots)

    def place(c, carry):
        cx, cz, cy = c // 8, lax.rem(c // 4, 2), lax.rem(c, 4)
        part[0, cy, cx, cz] = run[ending(3, c * 2)]
        part[1, cx, cy, cz] = run[ending(3, c * 2 + 1)]
        return carry

    lax.fori_loop(0, 32, place, 0)

    big, small = (y, x), (x, y)
    at_big, at_small = (at_y, at_x), (at_x, at_y)
    layers = (1 - zh, zh)
    both = (0, 1)
    copies = {}

    def issue(n, lay):
        for h in both:
            q = step4(small[h], OFFSETS[n])
            for d in (2, 1, 3):
                src = part.at[h, step4(big[h], d), q, layers[lay]]
                send(src, landed.at[h, lay, n, d - 1], at_big[h](d), ("big", h, lay, n), 1 + lay)

    def finish(n, lay):
        for h in both:
            q = step4(small[h], OFFSETS[n])
            wait_all(landed.at[h, lay, n], arrival(("big", h, lay, n)))
            total = part[h, big[h], q, layers[lay]].astype(F32)
            for d in (2, 1, 3):
                total = total + landed[h, lay, n, d - 1].astype(F32)
            if n < 3:
                quarter[h, lay, n] = total.astype(BF16)
                src, dst = quarter.at[h, lay, n], landed_q.at[h, lay, n]
                send(src, dst, at_small[h](OFFSETS[n]), ("small", h, lay), 3)
            else:
                own_small[h, lay] = total

    def small_finish(lay):
        for h in both:
            wait_all(landed_q.at[h, lay], arrival(("small", h, lay)))
            total = own_small[h, lay]
            for n in range(3):
                total = total + landed_q[h, lay, n].astype(F32)
            if lay == 0:
                z_send[h] = total.astype(BF16)
                copies[h, "z"] = send(z_send.at[h], z_recv.at[h], z_peer, ("z", h), 3)
            else:
                halves[h] = total

    for n in range(4):
        issue(n, 0)
    for n in range(4):
        finish(n, 0)
        issue(n, 1)
    small_finish(0)
    for n in range(4):
        finish(n, 1)
    small_finish(1)

    weight_copy.wait()
    cot_copy.wait()
    bias_copy.wait()
    weight = weight_v[...]
    bias = bias_ref[...]

    def spread(h, off, lay):
        ref = grads.at[h, big[h], step4(small[h], off), layers[lay]]
        for d in (2, 1, 3):
            send(ref, ref, at_big[h](d), ("spread", lay), 4 + lay)

    def spread_small(h, lay):
        ref = grads.at[h, big[h], small[h], layers[lay]]
        for d in (2, 1, 3):
            copies[h, "p", lay, d] = send(ref, ref, at_small[h](d), ("pass", h, lay, d), 6)

    def pass_on(lay):
        for d in (1, 3, 2):
            for h in both:
                copies[h, "p", lay, d].wait_recv()
                spread(h, 4 - d, lay)

    for h in both:
        copies[h, "z"].wait_recv()
        hidden = scale_col[h] * (halves[h] + z_recv[h].astype(F32))
        upper, lower = two_parts(hidden)
        preact = dot(upper, weight) + dot(lower, weight) + bias
        gate = 1.0 / (1.0 + jnp.exp(-preact))
        rows = pl.ds(h * blk, blk)
        act_ref[rows, :] = (preact * gate).astype(BF16)
        grad_pre = cot_v[rows, :].astype(F32) * gate * (1.0 + preact * (1.0 - gate))
        hid_v[h] = hidden
        pre_v[h] = grad_pre
        upper, lower = two_parts(grad_pre)
        nt = ((1,), (1,))
        outgoing = scale_row[h] * (dot_general(weight, upper, nt) + dot_general(weight, lower, nt))
        grads[h, big[h], small[h], zh] = outgoing.astype(BF16)
        ref = grads.at[h, big[h], small[h], zh]
        copies[h, "g"] = send(ref, ref, z_peer, ("g", h), 3)
        spread_small(h, 1)
        spread(h, 0, 1)

    total = None
    bias_sum = None
    tn = ((0,), (0,))
    for h in both:
        hu, hl = two_parts(hid_v[h])
        gu, gl = two_parts(pre_v[h])
        term = dot_general(hu, gu, tn) + dot_general(hu, gl, tn) + dot_general(hl, gu, tn)
        sums = jnp.sum(pre_v[h], axis=0, keepdims=True)
        total = term if total is None else total + term
        bias_sum = sums if bias_sum is None else bias_sum + sums
    share = total.shape[0] // 8
    for r in range(8):
        gw_part[r % 2, r // 2, pl.ds(0, share), :] = total[r * share:(r + 1) * share, :]
        gw_part[r % 2, r // 2, pl.ds(share, 8), :] = jnp.broadcast_to(bias_sum, (8, bias_sum.shape[1]))
    gw_near = send(gw_part.at[1 - core], gw_in, sibling, "gw near", 7)

    gw_near.wait_recv()
    for z in range(4):
        gw_sum[z] = gw_part[core, z] + gw_in[z]
    gw_row[zl] = gw_sum[zl]
    for d in (1, 2, 3):
        other = step4(zl, d)
        send(gw_sum.at[other], gw_row.at[zl], at_row(other * 2 + core), "gw far", 8)
    pass_on(1)
    for h in both:
        copies[h, "g"].wait_recv()
        spread_small(h, 0)
        spread(h, 0, 0)
    wait_all(gw_row.at[pl.ds(0, 3)], arrival("gw far"))
    gw_z[zh] = gw_row[0] + gw_row[1] + gw_row[2] + gw_row[3]
    gw_across = send(gw_z.at[zh], gw_z.at[zh], z_peer, "gw z", 8)

    pass_on(0)

    def arrive(lay):
        wait_all(tiles.at[pl.ds(0, 24)], arrival(("spread", lay)))

    gw_across.wait_recv()
    gw_x[x] = gw_z[0] + gw_z[1]
    for d in (1, 2, 3):
        send(gw_x.at[x], gw_x.at[x], at_x(d), "gw x", 8)
    arrive(1)
    wait_all(gw_x.at[pl.ds(0, 3)], arrival("gw x"))
    gw_y[y] = gw_x[0] + gw_x[1] + gw_x[2] + gw_x[3]
    for d in (1, 2, 3):
        send(gw_y.at[y], gw_y.at[y], at_y(d), "gw y", 8)
    arrive(0)

    def backward(g, acc):
        steps = [g * UNROLL + u for u in range(UNROLL)]
        terms = [dot(flat_grad(table[5, p] & 63), tiles[table[4, p] & (slots - 1)]) for p in steps]
        for p, term in zip(steps, terms):
            acc = acc * table[6, p].astype(F32) + term
            run[p] = acc.astype(BF16)
        return acc

    def flat_grad(s):
        return grads[s // 32, lax.rem(s // 8, 4), lax.rem(s // 2, 4), lax.rem(s, 2)]

    zero_t = jnp.zeros((run.shape[1], blk), F32)
    lax.fori_loop(0, slots // UNROLL, backward, zero_t)
    wait_all(gw_y.at[pl.ds(0, 3)], arrival("gw y"))
    piece = gw_y[0] + gw_y[1] + gw_y[2] + gw_y[3]
    gb_ref[...] = piece[share:share + 1, :]
    gw_all[row] = piece[:share, :].astype(BF16)
    mine = gw_all.at[row]
    for d in range(1, 8):
        send(mine, mine, at_row(lax.rem(row + d, 8)), "gw out", 10)

    def place_back(r, carry):
        for b in range(2):
            back[lax.rem(r, 2), r // 2, b] = run[ending(7, r * 2 + b)]
        return carry

    lax.fori_loop(0, 8, place_back, 0)

    near = []
    for d in (1, 2, 3, 0):
        other = step4(zl, d)
        near.append(send(back.at[1 - core, other], back_in.at[d], sibling, ("back", d), 9))
    for n, d in enumerate((1, 2, 3)):
        other = step4(zl, d)
        near[n].wait_recv()
        back_sum[n] = (back[core, other].astype(F32) + back_in[d].astype(F32)).astype(BF16)
        send(back_sum.at[n], back_recv.at[n], at_row(other * 2 + core), "back", 9)
    near[3].wait_recv()
    own = back[core, zl].astype(F32) + back_in[0].astype(F32)
    wait_all(gw_all.at[pl.ds(0, 7)], arrival("gw out"))
    for r in range(8):
        gw_ref[pl.ds(r * share, share), :] = gw_all[r].astype(F32)
    wait_all(back_recv, arrival("back"))
    for n in range(3):
        own = own + back_recv[n].astype(F32)
    for b in range(2):
        gf_ref[pl.ds(b * blk, blk), :] = jnp.transpose(scale_row[b] * own[b]).astype(BF16)

    assert len(slot_of) == ARRIVALS
    pairs = {0, 9}
    for lot, count in lots.items():
        if lot == 7:
            ref = gw_in
        elif lot == 8:
            ref = gw_wait.at[pl.ds(0, count)]
        elif lot == 10:
            ref = gw_all.at[pl.ds(0, count)]
        else:
            ref = tiles.at[pl.ds(0, count * 2 if lot in pairs else count)]
        wait_all(ref, send_sem.at[lot])


def deliver_kernel(*refs):
    sems = refs[8]
    moves = [pltpu.make_async_copy(refs[n], refs[n + 4], sems.at[n]) for n in range(4)]
    for move in moves:
        move.start()
    for move in moves:
        move.wait()


def per_device(
    features, weight, bias_vector, cotangent, degrees, adjacency_tiles, tile_positions, tile_counts
):
    slots, blk = adjacency_tiles.shape[2:4]
    f_in, hid = weight.shape
    nodes = features.shape[0]
    share = f_in // 8
    anywhere = pl.BlockSpec(memory_space=pl.ANY)
    piece = (share + 8, hid)
    vmem = pl.BlockSpec(memory_space=pltpu.VMEM)

    def in_hbm(value):
        return pltpu.with_memory_space_constraint(value, pltpu.HBM)

    outs = pl.pallas_call(
        layer_kernel,
        out_shape=(
            pltpu.VMEM((nodes, hid), BF16),
            pltpu.VMEM((nodes, f_in), BF16),
            pltpu.VMEM((f_in, hid), F32),
            pltpu.VMEM((1, hid), F32),
        ),
        in_specs=[anywhere] * 8,
        out_specs=(vmem,) * 4,
        scratch_shapes=[
            pltpu.VMEM((nodes, f_in), BF16),
            pltpu.VMEM((1, hid), F32),
            pltpu.VMEM((2, blk), I32),
            pltpu.VMEM((1, slots), I32),
            pltpu.VMEM((1, 1), I32),
            pltpu.VMEM((slots, blk, blk), BF16),
            pltpu.VMEM((f_in, hid), BF16),
            pltpu.VMEM((nodes, hid), BF16),
            pltpu.VMEM((8, slots), I32),
            pltpu.SMEM((8, slots), I32),
            pltpu.VMEM((16, blk, f_in), BF16),
            pltpu.VMEM((slots + 1, blk, f_in), BF16),
            pltpu.VMEM((2, 4, 4, 2, blk, f_in), BF16),
            pltpu.VMEM((2, 2, 4, 3, blk, f_in), BF16),
            pltpu.VMEM((2, 2, 3, blk, f_in), BF16),
            pltpu.VMEM((2, 2, blk, f_in), F32),
            pltpu.VMEM((2, 2, 3, blk, f_in), BF16),
            pltpu.VMEM((2, blk, f_in), F32),
            pltpu.VMEM((2, blk, f_in), BF16),
            pltpu.VMEM((2, blk, f_in), BF16),
            pltpu.VMEM((2, 4, 4, 2, f_in, blk), BF16),
            pltpu.VMEM((2, blk, f_in), F32),
            pltpu.VMEM((2, blk, hid), F32),
            pltpu.VMEM((2, 4, 2, f_in, blk), BF16),
            pltpu.VMEM((4, 2, f_in, blk), BF16),
            pltpu.VMEM((3, 2, f_in, blk), BF16),
            pltpu.VMEM((3, 2, f_in, blk), BF16),
            pltpu.VMEM((2, 4) + piece, F32),
            pltpu.VMEM((4,) + piece, F32),
            pltpu.VMEM((4,) + piece, F32),
            pltpu.VMEM((4,) + piece, F32),
            pltpu.VMEM((4,) + piece, F32),
            pltpu.VMEM((4,) + piece, F32),
            pltpu.VMEM((2,) + piece, F32),
            pltpu.VMEM((8, share, hid), BF16),
            pltpu.VMEM((10,) + piece, F32),
            pltpu.SemaphoreType.DMA((9,)),
            pltpu.SemaphoreType.DMA((LOTS,)),
            pltpu.SemaphoreType.DMA((ARRIVALS,)),
        ],
        compiler_params=pltpu.CompilerParams(
            collective_id=0, has_side_effects=True, vmem_limit_bytes=VMEM_BYTES
        ),
        name="graph_layer",
    )(
        in_hbm(features),
        in_hbm(weight),
        in_hbm(bias_vector.reshape(1, hid)),
        in_hbm(cotangent),
        in_hbm(degrees.reshape(2, blk)),
        in_hbm(adjacency_tiles.reshape(slots, blk, blk)),
        in_hbm(tile_positions.reshape(1, slots)),
        tile_counts,
    )
    activations, grad_features, grad_weight, grad_bias = pl.pallas_call(
        deliver_kernel,
        out_shape=tuple(pltpu.HBM(o.shape, o.dtype) for o in outs),
        in_specs=[vmem] * 4,
        out_specs=(pl.BlockSpec(memory_space=pltpu.HBM),) * 4,
        scratch_shapes=[pltpu.SemaphoreType.DMA((4,))],
        name="deliver",
    )(*(pltpu.with_memory_space_constraint(o, pltpu.VMEM) for o in outs))
    return activations, grad_features, grad_weight, grad_bias.reshape(hid)


def solution(mesh):
    placed = (
        P(("row", "col"), None),
        P(),
        P(),
        P(("row", "col"), None),
        P(("row", "col")),
        P("row", "col", None, None, None),
        P("row", "col", None),
        P("row", "col"),
    )
    return jax.shard_map(
        per_device,
        mesh=mesh,
        in_specs=placed,
        out_specs=(P(("row", "col"), None), P(("row", "col"), None), P(), P()),
        check_vma=False,
    )
```

```python
import jax
import jax.numpy as jnp
from jax import lax
from jax.experimental import pallas as pl
from jax.experimental.pallas import tpu as pltpu
from jax.sharding import PartitionSpec as P

MESH = pl.DeviceIdType.MESH
F32 = jnp.float32
BF16 = jnp.bfloat16
I32 = jnp.int32
UNROLL = 32
ARRIVALS = 61
LOTS = 11
OFFSETS = (2, 1, 3, 0)
RELAYED = {(0, 1): 1, (3, 1): 3, (1, 1): 1, (2, 1): 3, (0, 0): 1}
VMEM_BYTES = 40 * 1024 * 1024


def two_parts(values):
    upper = values.astype(BF16)
    return upper, (values - upper.astype(F32)).astype(BF16)


def dot(a, b):
    return jnp.dot(a, b, preferred_element_type=F32)


def dot_general(a, b, dims):
    return lax.dot_general(a, b, (dims, ((), ())), preferred_element_type=F32)


def segment_plan(key, shift, eye, lane2, sub2, slots):
    key_col = jnp.sum(jnp.where(eye, key.astype(F32), 0.0), axis=1, keepdims=True).astype(I32)
    less = key < key_col
    rank = jnp.sum(jnp.where(less, 1.0, 0.0), axis=1, keepdims=True).astype(I32)
    seg_col = key_col >> shift
    before = jnp.where(less, 1.0, 0.0) * jnp.where((key >> shift) == seg_col, 1.0, 0.0)
    same = jnp.max(before, axis=1, keepdims=True)
    perm = rank == lane2

    def permuted(column):
        return jnp.sum(jnp.where(perm, column, 0.0), axis=0, keepdims=True).astype(I32)

    order = permuted(sub2.astype(F32))
    sorted_key = permuted(key_col.astype(F32))
    sorted_same = permuted(same)
    upto = jnp.sum(jnp.where(seg_col <= lane2, 1.0, 0.0), axis=0, keepdims=True).astype(I32)
    here = jnp.sum(jnp.where(seg_col == lane2, 1.0, 0.0), axis=0, keepdims=True).astype(I32)
    last = jnp.where(here > 0, upto - 1, slots)
    return order, sorted_key, sorted_same, last


def layer_kernel(
    feat_hbm, weight_hbm, bias_hbm, cot_hbm, deg_hbm, tiles_hbm, pos_hbm, cnt_hbm,
    act_ref, gf_ref, gw_ref, gb_ref,
    feat_ref, bias_ref, deg_ref, pos_ref, cnt_ref,
    tiles, weight_v, cot_v, table_v, table, gathered, run, part, landed, quarter, own_small,
    landed_q, halves, z_send, z_recv, grads, hid_v, pre_v, back, back_in, back_sum, back_recv,
    gw_part, gw_in, gw_sum, gw_row, gw_x, gw_y, gw_z, gw_all, gw_wait, local_sem, send_sem, recv_sem, feat_sem,
):
    slots, blk, _ = tiles.shape
    row = lax.axis_index("row")
    col = lax.axis_index("col")
    core = lax.rem(row, 2)
    zl = row // 2
    x = col // 8
    zh = lax.rem(col // 4, 2)
    y = lax.rem(col, 4)

    def step4(v, d):
        return lax.rem(v + d, 4)

    def at_x(d):
        return (row, step4(x, d) * 8 + zh * 4 + y)

    def at_y(d):
        return (row, x * 8 + zh * 4 + step4(y, d))

    def at_row(other):
        return (other, col)

    half = zl // 2
    chips = (3 - 3 * half, 2 - half, zl + 1 - 2 * lax.rem(zl, 2))
    z_peer = (row, x * 8 + (1 - zh) * 4 + y)
    sibling = at_row(zl * 2 + 1 - core)

    barrier = pltpu.get_barrier_semaphore()
    peers = [at_x(d) for d in (1, 2, 3)] + [at_y(d) for d in (1, 2, 3)] + [z_peer]
    peers += [at_row(other * 2 + core) for other in chips] + [sibling]
    for peer in peers:
        pl.semaphore_signal(barrier, inc=1, device_id=peer, device_id_type=MESH)

    def bring(n, src, dst):
        copy = pltpu.make_async_copy(src, dst, local_sem.at[n])
        copy.start()
        return copy

    pos_copy = bring(0, pos_hbm, pos_ref)
    cnt_copy = bring(8, cnt_hbm, cnt_ref)
    deg_copy = bring(1, deg_hbm, deg_ref)
    feat_copy = bring(2, feat_hbm, feat_ref)
    tiles_copy = bring(3, tiles_hbm, tiles)
    weight_copy = bring(4, weight_hbm, weight_v)
    cot_copy = bring(5, cot_hbm, cot_v)
    bias_copy = bring(6, bias_hbm, bias_ref)

    pos_copy.wait()
    cnt_copy.wait()
    pos = pos_ref[...]
    lane = lax.broadcasted_iota(I32, (1, slots), 1)
    live = lane < cnt_ref[...]
    lane2 = lax.broadcasted_iota(I32, (slots, slots), 1)
    sub2 = lax.broadcasted_iota(I32, (slots, slots), 0)
    eye = lane2 == sub2
    key_f = jnp.where(live, pos, 1024 + lane)
    key_b = jnp.where(live, (pos & 15) * 64 + (pos >> 4), 1024 + lane)
    order_f, sorted_f, same_f, last_f = segment_plan(key_f, 4, eye, lane2, sub2, slots)
    order_b, sorted_b, same_b, last_b = segment_plan(key_b, 6, eye, lane2, sub2, slots)
    rb = sorted_b & 63
    rb_x, rb_z, rb_y = rb >> 4, (rb >> 3) & 1, (rb >> 1) & 3
    slot_b = jnp.where((rb & 1) == 0, (rb_y * 4 + rb_x) * 2 + rb_z, 32 + (rb_x * 4 + rb_y) * 2 + rb_z)
    for n, line in enumerate((order_f, sorted_f & 15, same_f, last_f, order_b, slot_b, same_b, last_b)):
        table_v[pl.ds(n, 1), :] = line
    table_copy = bring(7, table_v, table)
    run[slots] = jnp.zeros((blk, run.shape[2]), BF16)

    deg_copy.wait()
    feat_copy.wait()
    eye_b = lax.broadcasted_iota(I32, (blk, blk), 0) == lax.broadcasted_iota(I32, (blk, blk), 1)
    scale_row = [lax.rsqrt(deg_ref[pl.ds(b, 1), :].astype(F32)) for b in range(2)]
    scale_col = [jnp.sum(jnp.where(eye_b, s, 0.0), axis=1, keepdims=True) for s in scale_row]
    for b in range(2):
        rows = pl.ds(b * blk, blk)
        gathered[row * 2 + b] = (scale_col[b] * feat_ref[rows, :].astype(F32)).astype(BF16)

    pl.semaphore_wait(barrier, len(peers))

    slot_of, lots = {}, {}

    def arrival(key, chip=None):
        if chip is not None:
            return feat_sem.at[chip]
        return recv_sem.at[slot_of.setdefault(key, len(slot_of))]

    def send(src, dst, device, key, lot, chip=None):
        copy = pltpu.make_async_remote_copy(
            src_ref=src, dst_ref=dst, send_sem=send_sem.at[lot], recv_sem=arrival(key, chip),
            device_id=device, device_id_type=MESH,
        )
        copy.start()
        lots[lot] = lots.get(lot, 0) + 1
        return copy

    def wait_all(ref, sem):
        pltpu.make_async_copy(ref, ref, sem).wait()

    def own_pair(r):
        return gathered.at[pl.ds(r * 2, 2)]

    mine = own_pair(row)
    for other in chips:
        send(mine, mine, at_row(other * 2 + core), "feat far", 0, zl)
    send(mine, mine, sibling, "feat", 0)

    for chip in (chips[2], chips[1], chips[0]):
        wait_all(mine, arrival("feat far", chip))
        other = chip * 2 + core
        send(own_pair(other), own_pair(other), sibling, "feat", 0)
    wait_all(gathered.at[pl.ds(0, 8)], arrival("feat"))

    table_copy.wait()
    tiles_copy.wait()

    def forward(g, acc):
        steps = [g * UNROLL + u for u in range(UNROLL)]
        terms = [dot(tiles[table[0, p] & (slots - 1)], gathered[table[1, p] & 15]) for p in steps]
        for p, term in zip(steps, terms):
            acc = acc * table[2, p].astype(F32) + term
            run[p] = acc.astype(BF16)
        return acc

    zero = jnp.zeros((blk, run.shape[2]), F32)
    lax.fori_loop(0, slots // UNROLL, forward, zero)

    def ending(line, segment):
        return jnp.clip(table[line, segment], 0, slots)

    def place(c, carry):
        cx, cz, cy = c // 8, lax.rem(c // 4, 2), lax.rem(c, 4)
        part[0, cy, cx, cz] = run[ending(3, c * 2)]
        part[1, cx, cy, cz] = run[ending(3, c * 2 + 1)]
        return carry

    lax.fori_loop(0, 32, place, 0)

    big, small = (y, x), (x, y)
    at_big, at_small = (at_y, at_x), (at_x, at_y)
    layers = (1 - zh, zh)
    both = (0, 1)
    copies = {}

    def issue(n, lay):
        for h in both:
            q = step4(small[h], OFFSETS[n])
            for d in (2, 1, 3):
                src = part.at[h, step4(big[h], d), q, layers[lay]]
                send(src, landed.at[h, lay, n, d - 1], at_big[h](d), ("big", h, lay, n), 1 + lay)

    def finish(n, lay):
        for h in both:
            q = step4(small[h], OFFSETS[n])
            wait_all(landed.at[h, lay, n], arrival(("big", h, lay, n)))
            total = part[h, big[h], q, layers[lay]].astype(F32)
            for d in (2, 1, 3):
                total = total + landed[h, lay, n, d - 1].astype(F32)
            if n < 3:
                quarter[h, lay, n] = total.astype(BF16)
                src, dst = quarter.at[h, lay, n], landed_q.at[h, lay, n]
                send(src, dst, at_small[h](OFFSETS[n]), ("small", h, lay), 3)
            else:
                own_small[h, lay] = total

    def small_finish(lay):
        for h in both:
            wait_all(landed_q.at[h, lay], arrival(("small", h, lay)))
            total = own_small[h, lay]
            for n in range(3):
                total = total + landed_q[h, lay, n].astype(F32)
            if lay == 0:
                z_send[h] = total.astype(BF16)
                copies[h, "z"] = send(z_send.at[h], z_recv.at[h], z_peer, ("z", h), 3)
            else:
                halves[h] = total

    for n in range(4):
        issue(n, 0)
    for n in range(4):
        finish(n, 0)
        issue(n, 1)
    small_finish(0)
    for n in range(4):
        finish(n, 1)
    small_finish(1)

    weight_copy.wait()
    cot_copy.wait()
    bias_copy.wait()
    weight = weight_v[...]
    bias = bias_ref[...]

    def spread(h, off, lay):
        ref = grads.at[h, big[h], step4(small[h], off), layers[lay]]
        way = RELAYED.get((off, lay))
        for d in (1, 3) if way else (2, 1, 3):
            key = ("relay", h, off, lay) if d == way else ("spread", lay)
            copies[h, off, lay, d] = send(ref, ref, at_big[h](d), key, 4 + lay)

    def relay(off, lay):
        way = RELAYED[off, lay]
        for h in both:
            copies[h, off, lay, way].wait_recv()
            ref = grads.at[h, step4(big[h], 4 - way), step4(small[h], off), layers[lay]]
            send(ref, ref, at_big[h](way), ("spread", lay), 4 + lay)

    def spread_small(h, lay):
        ref = grads.at[h, big[h], small[h], layers[lay]]
        for d in (2, 1, 3):
            copies[h, "p", lay, d] = send(ref, ref, at_small[h](d), ("pass", h, lay, d), 6)

    def pass_on(lay):
        for d in (1, 3, 2):
            for h in both:
                copies[h, "p", lay, d].wait_recv()
                spread(h, 4 - d, lay)

    for h in both:
        copies[h, "z"].wait_recv()
        hidden = scale_col[h] * (halves[h] + z_recv[h].astype(F32))
        upper, lower = two_parts(hidden)
        preact = dot(upper, weight) + dot(lower, weight) + bias
        gate = 1.0 / (1.0 + jnp.exp(-preact))
        rows = pl.ds(h * blk, blk)
        act_ref[rows, :] = (preact * gate).astype(BF16)
        grad_pre = cot_v[rows, :].astype(F32) * gate * (1.0 + preact * (1.0 - gate))
        hid_v[h] = hidden
        pre_v[h] = grad_pre
        upper, lower = two_parts(grad_pre)
        nt = ((1,), (1,))
        outgoing = scale_row[h] * (dot_general(weight, upper, nt) + dot_general(weight, lower, nt))
        grads[h, big[h], small[h], zh] = outgoing.astype(BF16)
        ref = grads.at[h, big[h], small[h], zh]
        copies[h, "g"] = send(ref, ref, z_peer, ("g", h), 3)
        spread_small(h, 1)
        spread(h, 0, 1)

    total = None
    bias_sum = None
    tn = ((0,), (0,))
    for h in both:
        hu, hl = two_parts(hid_v[h])
        gu, gl = two_parts(pre_v[h])
        term = dot_general(hu, gu, tn) + dot_general(hu, gl, tn) + dot_general(hl, gu, tn)
        sums = jnp.sum(pre_v[h], axis=0, keepdims=True)
        total = term if total is None else total + term
        bias_sum = sums if bias_sum is None else bias_sum + sums
    share = total.shape[0] // 8
    for r in range(8):
        gw_part[r % 2, r // 2, pl.ds(0, share), :] = total[r * share:(r + 1) * share, :]
        gw_part[r % 2, r // 2, pl.ds(share, 8), :] = jnp.broadcast_to(bias_sum, (8, bias_sum.shape[1]))
    gw_near = send(gw_part.at[1 - core], gw_in, sibling, "gw near", 7)

    gw_near.wait_recv()
    for z in range(4):
        gw_sum[z] = gw_part[core, z] + gw_in[z]
    gw_row[zl] = gw_sum[zl]
    for d in (1, 2, 3):
        other = step4(zl, d)
        send(gw_sum.at[other], gw_row.at[zl], at_row(other * 2 + core), "gw far", 8)
    pass_on(1)
    relay(0, 1)
    for h in both:
        copies[h, "g"].wait_recv()
        spread_small(h, 0)
        spread(h, 0, 0)
    relay(3, 1)
    relay(1, 1)
    relay(2, 1)
    wait_all(gw_row.at[pl.ds(0, 3)], arrival("gw far"))
    gw_z[zh] = gw_row[0] + gw_row[1] + gw_row[2] + gw_row[3]
    gw_across = send(gw_z.at[zh], gw_z.at[zh], z_peer, "gw z", 8)

    pass_on(0)
    relay(0, 0)

    def arrive(lay):
        relayed = sum(1 for _, other in RELAYED if other == lay)
        wait_all(tiles.at[pl.ds(0, 24 - 2 * relayed)], arrival(("spread", lay)))

    gw_across.wait_recv()
    gw_x[x] = gw_z[0] + gw_z[1]
    for d in (1, 2, 3):
        send(gw_x.at[x], gw_x.at[x], at_x(d), "gw x", 8)
    arrive(1)
    arrive(0)

    def backward(g, acc):
        steps = [g * UNROLL + u for u in range(UNROLL)]
        terms = [dot(flat_grad(table[5, p] & 63), tiles[table[4, p] & (slots - 1)]) for p in steps]
        for p, term in zip(steps, terms):
            acc = acc * table[6, p].astype(F32) + term
            run[p] = acc.astype(BF16)
        return acc

    def flat_grad(s):
        return grads[s // 32, lax.rem(s // 8, 4), lax.rem(s // 2, 4), lax.rem(s, 2)]

    zero_t = jnp.zeros((run.shape[1], blk), F32)
    middle = slots // UNROLL // 2
    acc = lax.fori_loop(0, middle, backward, zero_t)
    wait_all(gw_x.at[pl.ds(0, 3)], arrival("gw x"))
    gw_y[y] = gw_x[0] + gw_x[1] + gw_x[2] + gw_x[3]
    for d in (1, 2, 3):
        send(gw_y.at[y], gw_y.at[y], at_y(d), "gw y", 8)
    lax.fori_loop(middle, slots // UNROLL, backward, acc)
    def place_back(r, carry):
        for b in range(2):
            back[lax.rem(r, 2), r // 2, b] = run[ending(7, r * 2 + b)]
        return carry

    lax.fori_loop(0, 8, place_back, 0)

    near = []
    for n, other in enumerate((*chips, zl)):
        near.append(send(back.at[1 - core, other], back_in.at[n], sibling, ("back", n), 9))
    wait_all(gw_y.at[pl.ds(0, 3)], arrival("gw y"))
    piece = gw_y[0] + gw_y[1] + gw_y[2] + gw_y[3]
    gb_ref[...] = piece[share:share + 1, :]
    gw_all[row] = piece[:share, :].astype(BF16)
    mine = gw_all.at[row]
    for other in chips:
        send(mine, mine, at_row(other * 2 + core), "gw out", 10)
    send(mine, mine, sibling, "gw pass", 10)

    for n, other in enumerate(chips):
        near[n].wait_recv()
        back_sum[n] = (back[core, other].astype(F32) + back_in[n].astype(F32)).astype(BF16)
        send(back_sum.at[n], back_recv.at[zl], at_row(other * 2 + core), "back", 9)
    near[3].wait_recv()
    own = back[core, zl].astype(F32) + back_in[3].astype(F32)
    wait_all(gw_all.at[pl.ds(0, 3)], arrival("gw out"))
    for chip in chips:
        passed = gw_all.at[chip * 2 + core]
        send(passed, passed, sibling, "gw pass", 10)
    wait_all(gw_all.at[pl.ds(0, 4)], arrival("gw pass"))
    for r in range(8):
        gw_ref[pl.ds(r * share, share), :] = gw_all[r].astype(F32)
    wait_all(back_recv.at[pl.ds(0, 3)], arrival("back"))
    for other in chips:
        own = own + back_recv[other].astype(F32)
    for b in range(2):
        gf_ref[pl.ds(b * blk, blk), :] = jnp.transpose(scale_row[b] * own[b]).astype(BF16)

    assert len(slot_of) == ARRIVALS
    pairs = {0, 9}
    for lot, count in lots.items():
        if lot == 7:
            ref = gw_in
        elif lot == 8:
            ref = gw_wait.at[pl.ds(0, count)]
        elif lot == 10:
            ref = gw_all.at[pl.ds(0, count)]
        else:
            ref = tiles.at[pl.ds(0, count * 2 if lot in pairs else count)]
        wait_all(ref, send_sem.at[lot])


def deliver_kernel(*refs):
    sems = refs[8]
    moves = [pltpu.make_async_copy(refs[n], refs[n + 4], sems.at[n]) for n in range(4)]
    for move in moves:
        move.start()
    for move in moves:
        move.wait()


def per_device(
    features, weight, bias_vector, cotangent, degrees, adjacency_tiles, tile_positions, tile_counts
):
    slots, blk = adjacency_tiles.shape[2:4]
    f_in, hid = weight.shape
    nodes = features.shape[0]
    share = f_in // 8
    anywhere = pl.BlockSpec(memory_space=pl.ANY)
    piece = (share + 8, hid)
    vmem = pl.BlockSpec(memory_space=pltpu.VMEM)

    def in_hbm(value):
        return pltpu.with_memory_space_constraint(value, pltpu.HBM)

    outs = pl.pallas_call(
        layer_kernel,
        out_shape=(
            pltpu.VMEM((nodes, hid), BF16),
            pltpu.VMEM((nodes, f_in), BF16),
            pltpu.VMEM((f_in, hid), F32),
            pltpu.VMEM((1, hid), F32),
        ),
        in_specs=[anywhere] * 8,
        out_specs=(vmem,) * 4,
        scratch_shapes=[
            pltpu.VMEM((nodes, f_in), BF16),
            pltpu.VMEM((1, hid), F32),
            pltpu.VMEM((2, blk), I32),
            pltpu.VMEM((1, slots), I32),
            pltpu.VMEM((1, 1), I32),
            pltpu.VMEM((slots, blk, blk), BF16),
            pltpu.VMEM((f_in, hid), BF16),
            pltpu.VMEM((nodes, hid), BF16),
            pltpu.VMEM((8, slots), I32),
            pltpu.SMEM((8, slots), I32),
            pltpu.VMEM((16, blk, f_in), BF16),
            pltpu.VMEM((slots + 1, blk, f_in), BF16),
            pltpu.VMEM((2, 4, 4, 2, blk, f_in), BF16),
            pltpu.VMEM((2, 2, 4, 3, blk, f_in), BF16),
            pltpu.VMEM((2, 2, 3, blk, f_in), BF16),
            pltpu.VMEM((2, 2, blk, f_in), F32),
            pltpu.VMEM((2, 2, 3, blk, f_in), BF16),
            pltpu.VMEM((2, blk, f_in), F32),
            pltpu.VMEM((2, blk, f_in), BF16),
            pltpu.VMEM((2, blk, f_in), BF16),
            pltpu.VMEM((2, 4, 4, 2, f_in, blk), BF16),
            pltpu.VMEM((2, blk, f_in), F32),
            pltpu.VMEM((2, blk, hid), F32),
            pltpu.VMEM((2, 4, 2, f_in, blk), BF16),
            pltpu.VMEM((4, 2, f_in, blk), BF16),
            pltpu.VMEM((3, 2, f_in, blk), BF16),
            pltpu.VMEM((4, 2, f_in, blk), BF16),
            pltpu.VMEM((2, 4) + piece, F32),
            pltpu.VMEM((4,) + piece, F32),
            pltpu.VMEM((4,) + piece, F32),
            pltpu.VMEM((4,) + piece, F32),
            pltpu.VMEM((4,) + piece, F32),
            pltpu.VMEM((4,) + piece, F32),
            pltpu.VMEM((2,) + piece, F32),
            pltpu.VMEM((8, share, hid), BF16),
            pltpu.VMEM((10,) + piece, F32),
            pltpu.SemaphoreType.DMA((9,)),
            pltpu.SemaphoreType.DMA((LOTS,)),
            pltpu.SemaphoreType.DMA((ARRIVALS,)),
            pltpu.SemaphoreType.DMA((4,)),
        ],
        compiler_params=pltpu.CompilerParams(
            collective_id=0, has_side_effects=True, vmem_limit_bytes=VMEM_BYTES
        ),
        name="graph_layer",
    )(
        in_hbm(features),
        in_hbm(weight),
        in_hbm(bias_vector.reshape(1, hid)),
        in_hbm(cotangent),
        in_hbm(degrees.reshape(2, blk)),
        in_hbm(adjacency_tiles.reshape(slots, blk, blk)),
        in_hbm(tile_positions.reshape(1, slots)),
        tile_counts,
    )
    activations, grad_features, grad_weight, grad_bias = pl.pallas_call(
        deliver_kernel,
        out_shape=tuple(pltpu.HBM(o.shape, o.dtype) for o in outs),
        in_specs=[vmem] * 4,
        out_specs=(pl.BlockSpec(memory_space=pltpu.HBM),) * 4,
        scratch_shapes=[pltpu.SemaphoreType.DMA((4,))],
        name="deliver",
    )(*(pltpu.with_memory_space_constraint(o, pltpu.VMEM) for o in outs))
    return activations, grad_features, grad_weight, grad_bias.reshape(hid)


def solution(mesh):
    placed = (
        P(("row", "col"), None),
        P(),
        P(),
        P(("row", "col"), None),
        P(("row", "col")),
        P("row", "col", None, None, None),
        P("row", "col", None),
        P("row", "col"),
    )
    return jax.shard_map(
        per_device,
        mesh=mesh,
        in_specs=placed,
        out_specs=(P(("row", "col"), None), P(("row", "col"), None), P(), P()),
        check_vma=False,
    )
```

```python
import jax
import jax.numpy as jnp
from jax import lax
from jax.experimental import pallas as pl
from jax.experimental.pallas import tpu as pltpu
from jax.sharding import PartitionSpec as P

MESH = pl.DeviceIdType.MESH
F32 = jnp.float32
BF16 = jnp.bfloat16
I32 = jnp.int32
UNROLL = 32
ARRIVALS = 61
LOTS = 11
OFFSETS = (2, 1, 3, 0)
RELAYED = {(0, 1): 1, (3, 1): 3, (1, 1): 1, (2, 1): 3, (0, 0): 1}
VMEM_BYTES = 40 * 1024 * 1024


def two_parts(values):
    upper = values.astype(BF16)
    return upper, (values - upper.astype(F32)).astype(BF16)


def dot(a, b):
    return jnp.dot(a, b, preferred_element_type=F32)


def dot_general(a, b, dims):
    return lax.dot_general(a, b, (dims, ((), ())), preferred_element_type=F32)


def segment_plan(key, shift, eye, lane2, sub2, slots):
    key_col = jnp.sum(jnp.where(eye, key.astype(F32), 0.0), axis=1, keepdims=True).astype(I32)
    less = key < key_col
    rank = jnp.sum(jnp.where(less, 1.0, 0.0), axis=1, keepdims=True).astype(I32)
    seg_col = key_col >> shift
    before = jnp.where(less, 1.0, 0.0) * jnp.where((key >> shift) == seg_col, 1.0, 0.0)
    same = jnp.max(before, axis=1, keepdims=True)
    perm = rank == lane2

    def permuted(column):
        return jnp.sum(jnp.where(perm, column, 0.0), axis=0, keepdims=True).astype(I32)

    order = permuted(sub2.astype(F32))
    sorted_key = permuted(key_col.astype(F32))
    sorted_same = permuted(same)
    upto = jnp.sum(jnp.where(seg_col <= lane2, 1.0, 0.0), axis=0, keepdims=True).astype(I32)
    here = jnp.sum(jnp.where(seg_col == lane2, 1.0, 0.0), axis=0, keepdims=True).astype(I32)
    last = jnp.where(here > 0, upto - 1, slots)
    return order, sorted_key, sorted_same, last


def layer_kernel(
    feat_hbm, weight_hbm, bias_hbm, cot_hbm, deg_hbm, tiles_hbm, pos_hbm, cnt_hbm,
    act_ref, gf_ref, gw_ref, gb_ref,
    feat_ref, bias_ref, deg_ref, pos_ref, cnt_ref,
    tiles, weight_v, cot_v, table_v, table, gathered, run, part, landed, quarter, own_small,
    landed_q, halves, z_send, z_recv, grads, hid_v, pre_v, back, back_in, back_sum, back_recv,
    gw_part, gw_in, gw_sum, gw_row, gw_x, gw_y, gw_z, gw_all, gw_wait, local_sem, send_sem, recv_sem, feat_sem,
):
    slots, blk, _ = tiles.shape
    row = lax.axis_index("row")
    col = lax.axis_index("col")
    core = lax.rem(row, 2)
    zl = row // 2
    x = col // 8
    zh = lax.rem(col // 4, 2)
    y = lax.rem(col, 4)

    def step4(v, d):
        return lax.rem(v + d, 4)

    def at_x(d):
        return (row, step4(x, d) * 8 + zh * 4 + y)

    def at_y(d):
        return (row, x * 8 + zh * 4 + step4(y, d))

    def at_row(other):
        return (other, col)

    half = zl // 2
    chips = (3 - 3 * half, 2 - half, zl + 1 - 2 * lax.rem(zl, 2))
    z_peer = (row, x * 8 + (1 - zh) * 4 + y)
    sibling = at_row(zl * 2 + 1 - core)

    barrier = pltpu.get_barrier_semaphore()
    peers = [at_x(d) for d in (1, 2, 3)] + [at_y(d) for d in (1, 2, 3)] + [z_peer]
    peers += [at_row(other * 2 + core) for other in chips] + [sibling]
    for peer in peers:
        pl.semaphore_signal(barrier, inc=1, device_id=peer, device_id_type=MESH)

    def bring(n, src, dst):
        copy = pltpu.make_async_copy(src, dst, local_sem.at[n])
        copy.start()
        return copy

    pos_copy = bring(0, pos_hbm, pos_ref)
    cnt_copy = bring(8, cnt_hbm, cnt_ref)
    deg_copy = bring(1, deg_hbm, deg_ref)
    feat_copy = bring(2, feat_hbm, feat_ref)
    tiles_copy = bring(3, tiles_hbm, tiles)
    weight_copy = bring(4, weight_hbm, weight_v)
    cot_copy = bring(5, cot_hbm, cot_v)
    bias_copy = bring(6, bias_hbm, bias_ref)

    pos_copy.wait()
    cnt_copy.wait()
    pos = pos_ref[...]
    lane = lax.broadcasted_iota(I32, (1, slots), 1)
    live = lane < cnt_ref[...]
    lane2 = lax.broadcasted_iota(I32, (slots, slots), 1)
    sub2 = lax.broadcasted_iota(I32, (slots, slots), 0)
    eye = lane2 == sub2
    key_f = jnp.where(live, pos, 1024 + lane)
    key_b = jnp.where(live, (pos & 15) * 64 + (pos >> 4), 1024 + lane)
    order_f, sorted_f, same_f, last_f = segment_plan(key_f, 4, eye, lane2, sub2, slots)
    order_b, sorted_b, same_b, last_b = segment_plan(key_b, 6, eye, lane2, sub2, slots)
    rb = sorted_b & 63
    rb_x, rb_z, rb_y = rb >> 4, (rb >> 3) & 1, (rb >> 1) & 3
    slot_b = jnp.where((rb & 1) == 0, (rb_y * 4 + rb_x) * 2 + rb_z, 32 + (rb_x * 4 + rb_y) * 2 + rb_z)
    for n, line in enumerate((order_f, sorted_f & 15, same_f, last_f, order_b, slot_b, same_b, last_b)):
        table_v[pl.ds(n, 1), :] = line
    table_copy = bring(7, table_v, table)
    run[slots] = jnp.zeros((blk, run.shape[2]), BF16)

    deg_copy.wait()
    feat_copy.wait()
    eye_b = lax.broadcasted_iota(I32, (blk, blk), 0) == lax.broadcasted_iota(I32, (blk, blk), 1)
    scale_row = [lax.rsqrt(deg_ref[pl.ds(b, 1), :].astype(F32)) for b in range(2)]
    scale_col = [jnp.sum(jnp.where(eye_b, s, 0.0), axis=1, keepdims=True) for s in scale_row]
    for b in range(2):
        rows = pl.ds(b * blk, blk)
        gathered[row * 2 + b] = (scale_col[b] * feat_ref[rows, :].astype(F32)).astype(BF16)

    pl.semaphore_wait(barrier, len(peers))

    slot_of, lots = {}, {}

    def arrival(key, chip=None):
        if chip is not None:
            return feat_sem.at[chip]
        return recv_sem.at[slot_of.setdefault(key, len(slot_of))]

    def send(src, dst, device, key, lot, chip=None):
        copy = pltpu.make_async_remote_copy(
            src_ref=src, dst_ref=dst, send_sem=send_sem.at[lot], recv_sem=arrival(key, chip),
            device_id=device, device_id_type=MESH,
        )
        copy.start()
        lots[lot] = lots.get(lot, 0) + 1
        return copy

    def wait_all(ref, sem):
        pltpu.make_async_copy(ref, ref, sem).wait()

    def own_pair(r):
        return gathered.at[pl.ds(r * 2, 2)]

    mine = own_pair(row)
    for other in chips:
        send(mine, mine, at_row(other * 2 + core), "feat far", 0, zl)
    send(mine, mine, sibling, "feat", 0)

    for chip in (chips[2], chips[1], chips[0]):
        wait_all(mine, arrival("feat far", chip))
        other = chip * 2 + core
        send(own_pair(other), own_pair(other), sibling, "feat", 0)
    wait_all(gathered.at[pl.ds(0, 8)], arrival("feat"))

    table_copy.wait()
    tiles_copy.wait()

    def forward(g, acc):
        steps = [g * UNROLL + u for u in range(UNROLL)]
        terms = [dot(tiles[table[0, p] & (slots - 1)], gathered[table[1, p] & 15]) for p in steps]
        for p, term in zip(steps, terms):
            acc = acc * table[2, p].astype(F32) + term
            run[p] = acc.astype(BF16)
        return acc

    zero = jnp.zeros((blk, run.shape[2]), F32)
    lax.fori_loop(0, slots // UNROLL, forward, zero)

    def ending(line, segment):
        return jnp.clip(table[line, segment], 0, slots)

    big, small = (y, x), (x, y)
    at_big, at_small = (at_y, at_x), (at_x, at_y)
    layers = (1 - zh, zh)
    both = (0, 1)
    copies = {}

    def issue(n, lay):
        for h in both:
            q = step4(small[h], OFFSETS[n])
            for c in range(4):
                device = (q * 8 + c if h == 0 else c * 8 + q) + layers[lay] * 4
                part[h, c, q, layers[lay]] = run[ending(3, device * 2 + h)]
            for d in (2, 1, 3):
                src = part.at[h, step4(big[h], d), q, layers[lay]]
                send(src, landed.at[h, lay, n, d - 1], at_big[h](d), ("big", h, lay, n), 1 + lay)

    def finish(n, lay):
        for h in both:
            q = step4(small[h], OFFSETS[n])
            wait_all(landed.at[h, lay, n], arrival(("big", h, lay, n)))
            total = part[h, big[h], q, layers[lay]].astype(F32)
            for d in (2, 1, 3):
                total = total + landed[h, lay, n, d - 1].astype(F32)
            if n < 3:
                quarter[h, lay, n] = total.astype(BF16)
                src, dst = quarter.at[h, lay, n], landed_q.at[h, lay, n]
                send(src, dst, at_small[h](OFFSETS[n]), ("small", h, lay), 3)
            else:
                own_small[h, lay] = total

    def small_finish(lay):
        for h in both:
            wait_all(landed_q.at[h, lay], arrival(("small", h, lay)))
            total = own_small[h, lay]
            for n in range(3):
                total = total + landed_q[h, lay, n].astype(F32)
            if lay == 0:
                z_send[h] = total.astype(BF16)
                copies[h, "z"] = send(z_send.at[h], z_recv.at[h], z_peer, ("z", h), 3)
            else:
                halves[h] = total

    for n in range(4):
        issue(n, 0)
    for n in range(4):
        finish(n, 0)
        issue(n, 1)
    small_finish(0)
    for n in range(4):
        finish(n, 1)
    small_finish(1)

    weight_copy.wait()
    cot_copy.wait()
    bias_copy.wait()
    weight = weight_v[...]
    bias = bias_ref[...]

    def spread(h, off, lay):
        ref = grads.at[h, big[h], step4(small[h], off), layers[lay]]
        way = RELAYED.get((off, lay))
        for d in (1, 3) if way else (2, 1, 3):
            key = ("relay", h, off, lay) if d == way else ("spread", lay)
            copies[h, off, lay, d] = send(ref, ref, at_big[h](d), key, 4 + lay)

    def relay(off, lay):
        way = RELAYED[off, lay]
        for h in both:
            copies[h, off, lay, way].wait_recv()
            ref = grads.at[h, step4(big[h], 4 - way), step4(small[h], off), layers[lay]]
            send(ref, ref, at_big[h](way), ("spread", lay), 4 + lay)

    def spread_small(h, lay):
        ref = grads.at[h, big[h], small[h], layers[lay]]
        for d in (2, 1, 3):
            copies[h, "p", lay, d] = send(ref, ref, at_small[h](d), ("pass", h, lay, d), 6)

    def pass_on(lay):
        for d in (1, 3, 2):
            for h in both:
                copies[h, "p", lay, d].wait_recv()
                spread(h, 4 - d, lay)

    for h in both:
        copies[h, "z"].wait_recv()
        hidden = scale_col[h] * (halves[h] + z_recv[h].astype(F32))
        upper, lower = two_parts(hidden)
        preact = dot(upper, weight) + dot(lower, weight) + bias
        gate = 1.0 / (1.0 + jnp.exp(-preact))
        rows = pl.ds(h * blk, blk)
        act_ref[rows, :] = (preact * gate).astype(BF16)
        grad_pre = cot_v[rows, :].astype(F32) * gate * (1.0 + preact * (1.0 - gate))
        hid_v[h] = hidden
        pre_v[h] = grad_pre
        upper, lower = two_parts(grad_pre)
        nt = ((1,), (1,))
        outgoing = scale_row[h] * (dot_general(weight, upper, nt) + dot_general(weight, lower, nt))
        grads[h, big[h], small[h], zh] = outgoing.astype(BF16)
        ref = grads.at[h, big[h], small[h], zh]
        copies[h, "g"] = send(ref, ref, z_peer, ("g", h), 3)
        spread_small(h, 1)
        spread(h, 0, 1)

    total = None
    bias_sum = None
    tn = ((0,), (0,))
    for h in both:
        hu, hl = two_parts(hid_v[h])
        gu, gl = two_parts(pre_v[h])
        term = dot_general(hu, gu, tn) + dot_general(hu, gl, tn) + dot_general(hl, gu, tn)
        sums = jnp.sum(pre_v[h], axis=0, keepdims=True)
        total = term if total is None else total + term
        bias_sum = sums if bias_sum is None else bias_sum + sums
    share = total.shape[0] // 8
    for r in range(8):
        gw_part[r % 2, r // 2, pl.ds(0, share), :] = total[r * share:(r + 1) * share, :]
        gw_part[r % 2, r // 2, pl.ds(share, 8), :] = jnp.broadcast_to(bias_sum, (8, bias_sum.shape[1]))
    gw_near = send(gw_part.at[1 - core], gw_in, sibling, "gw near", 7)

    gw_near.wait_recv()
    for z in range(4):
        gw_sum[z] = gw_part[core, z] + gw_in[z]
    gw_row[zl] = gw_sum[zl]
    for d in (1, 2, 3):
        other = step4(zl, d)
        send(gw_sum.at[other], gw_row.at[zl], at_row(other * 2 + core), "gw far", 8)
    pass_on(1)
    relay(0, 1)
    for h in both:
        copies[h, "g"].wait_recv()
        spread_small(h, 0)
        spread(h, 0, 0)
    relay(3, 1)
    relay(1, 1)
    relay(2, 1)
    wait_all(gw_row.at[pl.ds(0, 3)], arrival("gw far"))
    gw_z[zh] = gw_row[0] + gw_row[1] + gw_row[2] + gw_row[3]
    gw_across = send(gw_z.at[zh], gw_z.at[zh], z_peer, "gw z", 8)

    pass_on(0)
    relay(0, 0)

    def arrive(lay):
        relayed = sum(1 for _, other in RELAYED if other == lay)
        wait_all(tiles.at[pl.ds(0, 24 - 2 * relayed)], arrival(("spread", lay)))

    gw_across.wait_recv()
    gw_x[x] = gw_z[0] + gw_z[1]
    for d in (1, 2, 3):
        send(gw_x.at[x], gw_x.at[x], at_x(d), "gw x", 8)
    arrive(1)
    arrive(0)

    def backward(g, acc):
        steps = [g * UNROLL + u for u in range(UNROLL)]
        terms = [dot(flat_grad(table[5, p] & 63), tiles[table[4, p] & (slots - 1)]) for p in steps]
        for p, term in zip(steps, terms):
            acc = acc * table[6, p].astype(F32) + term
            run[p] = acc.astype(BF16)
        return acc

    def flat_grad(s):
        return grads[s // 32, lax.rem(s // 8, 4), lax.rem(s // 2, 4), lax.rem(s, 2)]

    zero_t = jnp.zeros((run.shape[1], blk), F32)
    middle = slots // UNROLL // 2
    acc = lax.fori_loop(0, middle, backward, zero_t)
    wait_all(gw_x.at[pl.ds(0, 3)], arrival("gw x"))
    gw_y[y] = gw_x[0] + gw_x[1] + gw_x[2] + gw_x[3]
    for d in (1, 2, 3):
        send(gw_y.at[y], gw_y.at[y], at_y(d), "gw y", 8)
    lax.fori_loop(middle, slots // UNROLL, backward, acc)
    def place_back(c, z):
        for b in range(2):
            back[c, z, b] = run[ending(7, z * 4 + c * 2 + b)]

    near = []
    for n, other in enumerate((*chips, zl)):
        place_back(1 - core, other)
        near.append(send(back.at[1 - core, other], back_in.at[n], sibling, ("back", n), 9))
    wait_all(gw_y.at[pl.ds(0, 3)], arrival("gw y"))
    piece = gw_y[0] + gw_y[1] + gw_y[2] + gw_y[3]
    gb_ref[...] = piece[share:share + 1, :]
    gw_all[row] = piece[:share, :].astype(BF16)
    mine = gw_all.at[row]
    for other in chips:
        send(mine, mine, at_row(other * 2 + core), "gw out", 10)
    send(mine, mine, sibling, "gw pass", 10)

    for other in (*chips, zl):
        place_back(core, other)
    for n, other in enumerate(chips):
        near[n].wait_recv()
        back_sum[n] = (back[core, other].astype(F32) + back_in[n].astype(F32)).astype(BF16)
        send(back_sum.at[n], back_recv.at[zl], at_row(other * 2 + core), "back", 9)
    near[3].wait_recv()
    own = back[core, zl].astype(F32) + back_in[3].astype(F32)
    wait_all(gw_all.at[pl.ds(0, 3)], arrival("gw out"))
    for chip in chips:
        passed = gw_all.at[chip * 2 + core]
        send(passed, passed, sibling, "gw pass", 10)
    wait_all(gw_all.at[pl.ds(0, 4)], arrival("gw pass"))
    for r in range(8):
        gw_ref[pl.ds(r * share, share), :] = gw_all[r].astype(F32)
    wait_all(back_recv.at[pl.ds(0, 3)], arrival("back"))
    for other in chips:
        own = own + back_recv[other].astype(F32)
    for b in range(2):
        gf_ref[pl.ds(b * blk, blk), :] = jnp.transpose(scale_row[b] * own[b]).astype(BF16)

    assert len(slot_of) == ARRIVALS
    pairs = {0, 9}
    for lot, count in lots.items():
        if lot == 7:
            ref = gw_in
        elif lot == 8:
            ref = gw_wait.at[pl.ds(0, count)]
        elif lot == 10:
            ref = gw_all.at[pl.ds(0, count)]
        else:
            ref = tiles.at[pl.ds(0, count * 2 if lot in pairs else count)]
        wait_all(ref, send_sem.at[lot])


def deliver_kernel(*refs):
    sems = refs[8]
    moves = [pltpu.make_async_copy(refs[n], refs[n + 4], sems.at[n]) for n in range(4)]
    for move in moves:
        move.start()
    for move in moves:
        move.wait()


def per_device(
    features, weight, bias_vector, cotangent, degrees, adjacency_tiles, tile_positions, tile_counts
):
    slots, blk = adjacency_tiles.shape[2:4]
    f_in, hid = weight.shape
    nodes = features.shape[0]
    share = f_in // 8
    anywhere = pl.BlockSpec(memory_space=pl.ANY)
    piece = (share + 8, hid)
    vmem = pl.BlockSpec(memory_space=pltpu.VMEM)

    def in_hbm(value):
        return pltpu.with_memory_space_constraint(value, pltpu.HBM)

    outs = pl.pallas_call(
        layer_kernel,
        out_shape=(
            pltpu.VMEM((nodes, hid), BF16),
            pltpu.VMEM((nodes, f_in), BF16),
            pltpu.VMEM((f_in, hid), F32),
            pltpu.VMEM((1, hid), F32),
        ),
        in_specs=[anywhere] * 8,
        out_specs=(vmem,) * 4,
        scratch_shapes=[
            pltpu.VMEM((nodes, f_in), BF16),
            pltpu.VMEM((1, hid), F32),
            pltpu.VMEM((2, blk), I32),
            pltpu.VMEM((1, slots), I32),
            pltpu.VMEM((1, 1), I32),
            pltpu.VMEM((slots, blk, blk), BF16),
            pltpu.VMEM((f_in, hid), BF16),
            pltpu.VMEM((nodes, hid), BF16),
            pltpu.VMEM((8, slots), I32),
            pltpu.SMEM((8, slots), I32),
            pltpu.VMEM((16, blk, f_in), BF16),
            pltpu.VMEM((slots + 1, blk, f_in), BF16),
            pltpu.VMEM((2, 4, 4, 2, blk, f_in), BF16),
            pltpu.VMEM((2, 2, 4, 3, blk, f_in), BF16),
            pltpu.VMEM((2, 2, 3, blk, f_in), BF16),
            pltpu.VMEM((2, 2, blk, f_in), F32),
            pltpu.VMEM((2, 2, 3, blk, f_in), BF16),
            pltpu.VMEM((2, blk, f_in), F32),
            pltpu.VMEM((2, blk, f_in), BF16),
            pltpu.VMEM((2, blk, f_in), BF16),
            pltpu.VMEM((2, 4, 4, 2, f_in, blk), BF16),
            pltpu.VMEM((2, blk, f_in), F32),
            pltpu.VMEM((2, blk, hid), F32),
            pltpu.VMEM((2, 4, 2, f_in, blk), BF16),
            pltpu.VMEM((4, 2, f_in, blk), BF16),
            pltpu.VMEM((3, 2, f_in, blk), BF16),
            pltpu.VMEM((4, 2, f_in, blk), BF16),
            pltpu.VMEM((2, 4) + piece, F32),
            pltpu.VMEM((4,) + piece, F32),
            pltpu.VMEM((4,) + piece, F32),
            pltpu.VMEM((4,) + piece, F32),
            pltpu.VMEM((4,) + piece, F32),
            pltpu.VMEM((4,) + piece, F32),
            pltpu.VMEM((2,) + piece, F32),
            pltpu.VMEM((8, share, hid), BF16),
            pltpu.VMEM((10,) + piece, F32),
            pltpu.SemaphoreType.DMA((9,)),
            pltpu.SemaphoreType.DMA((LOTS,)),
            pltpu.SemaphoreType.DMA((ARRIVALS,)),
            pltpu.SemaphoreType.DMA((4,)),
        ],
        compiler_params=pltpu.CompilerParams(
            collective_id=0, has_side_effects=True, vmem_limit_bytes=VMEM_BYTES
        ),
        name="graph_layer",
    )(
        in_hbm(features),
        in_hbm(weight),
        in_hbm(bias_vector.reshape(1, hid)),
        in_hbm(cotangent),
        in_hbm(degrees.reshape(2, blk)),
        in_hbm(adjacency_tiles.reshape(slots, blk, blk)),
        in_hbm(tile_positions.reshape(1, slots)),
        tile_counts,
    )
    activations, grad_features, grad_weight, grad_bias = pl.pallas_call(
        deliver_kernel,
        out_shape=tuple(pltpu.HBM(o.shape, o.dtype) for o in outs),
        in_specs=[vmem] * 4,
        out_specs=(pl.BlockSpec(memory_space=pltpu.HBM),) * 4,
        scratch_shapes=[pltpu.SemaphoreType.DMA((4,))],
        name="deliver",
    )(*(pltpu.with_memory_space_constraint(o, pltpu.VMEM) for o in outs))
    return activations, grad_features, grad_weight, grad_bias.reshape(hid)


def solution(mesh):
    placed = (
        P(("row", "col"), None),
        P(),
        P(),
        P(("row", "col"), None),
        P(("row", "col")),
        P("row", "col", None, None, None),
        P("row", "col", None),
        P("row", "col"),
    )
    return jax.shard_map(
        per_device,
        mesh=mesh,
        in_specs=placed,
        out_specs=(P(("row", "col"), None), P(("row", "col"), None), P(), P()),
        check_vma=False,
    )
```

```python
import jax
import jax.numpy as jnp
from jax import lax
from jax.experimental import pallas as pl
from jax.experimental.pallas import tpu as pltpu
from jax.sharding import PartitionSpec as P

MESH = pl.DeviceIdType.MESH
F32 = jnp.float32
BF16 = jnp.bfloat16
I32 = jnp.int32
UNROLL = 32
ARRIVALS = 61
LOTS = 11
OFFSETS = (2, 1, 3, 0)
RELAYED = {(0, 1): 1, (3, 1): 3, (1, 1): 1, (2, 1): 3, (0, 0): 1}
VMEM_BYTES = 40 * 1024 * 1024


def two_parts(values):
    upper = values.astype(BF16)
    return upper, (values - upper.astype(F32)).astype(BF16)


def dot(a, b):
    return jnp.dot(a, b, preferred_element_type=F32)


def dot_general(a, b, dims):
    return lax.dot_general(a, b, (dims, ((), ())), preferred_element_type=F32)


def segment_plan(key, shift, eye, lane2, sub2, slots):
    key_col = jnp.sum(jnp.where(eye, key.astype(F32), 0.0), axis=1, keepdims=True).astype(I32)
    less = key < key_col
    rank = jnp.sum(jnp.where(less, 1.0, 0.0), axis=1, keepdims=True).astype(I32)
    seg_col = key_col >> shift
    before = jnp.where(less, 1.0, 0.0) * jnp.where((key >> shift) == seg_col, 1.0, 0.0)
    same = jnp.max(before, axis=1, keepdims=True)
    perm = rank == lane2

    def permuted(column):
        return jnp.sum(jnp.where(perm, column, 0.0), axis=0, keepdims=True).astype(I32)

    order = permuted(sub2.astype(F32))
    sorted_key = permuted(key_col.astype(F32))
    sorted_same = permuted(same)
    upto = jnp.sum(jnp.where(seg_col <= lane2, 1.0, 0.0), axis=0, keepdims=True).astype(I32)
    here = jnp.sum(jnp.where(seg_col == lane2, 1.0, 0.0), axis=0, keepdims=True).astype(I32)
    last = jnp.where(here > 0, upto - 1, slots)
    return order, sorted_key, sorted_same, last


def layer_kernel(
    feat_hbm, weight_hbm, bias_hbm, cot_hbm, deg_hbm, tiles_hbm, pos_hbm, cnt_hbm,
    act_ref, gf_ref, gw_ref, gb_ref,
    feat_ref, bias_ref, deg_ref, pos_ref, cnt_ref,
    tiles, weight_v, cot_v, table_v, table, gathered, run, part, landed, quarter, own_small,
    landed_q, halves, z_send, z_recv, grads, hid_v, pre_v, back, back_in, back_sum, back_recv,
    gw_part, gw_in, gw_sum, gw_row, gw_x, gw_y, gw_z, gw_all, gw_wait, local_sem, send_sem, recv_sem, feat_sem,
):
    slots, blk, _ = tiles.shape
    row = lax.axis_index("row")
    col = lax.axis_index("col")
    core = lax.rem(row, 2)
    zl = row // 2
    x = col // 8
    zh = lax.rem(col // 4, 2)
    y = lax.rem(col, 4)

    def step4(v, d):
        return lax.rem(v + d, 4)

    def at_x(d):
        return (row, step4(x, d) * 8 + zh * 4 + y)

    def at_y(d):
        return (row, x * 8 + zh * 4 + step4(y, d))

    def at_row(other):
        return (other, col)

    half = zl // 2
    chips = (3 - 3 * half, 2 - half, zl + 1 - 2 * lax.rem(zl, 2))
    z_peer = (row, x * 8 + (1 - zh) * 4 + y)
    sibling = at_row(zl * 2 + 1 - core)

    barrier = pltpu.get_barrier_semaphore()
    peers = [at_x(d) for d in (1, 2, 3)] + [at_y(d) for d in (1, 2, 3)] + [z_peer]
    peers += [at_row(other * 2 + core) for other in chips] + [sibling]
    for peer in peers:
        pl.semaphore_signal(barrier, inc=1, device_id=peer, device_id_type=MESH)

    def bring(n, src, dst):
        copy = pltpu.make_async_copy(src, dst, local_sem.at[n])
        copy.start()
        return copy

    pos_copy = bring(0, pos_hbm, pos_ref)
    cnt_copy = bring(8, cnt_hbm, cnt_ref)
    deg_copy = bring(1, deg_hbm, deg_ref)
    feat_copy = bring(2, feat_hbm, feat_ref)
    tiles_copy = bring(3, tiles_hbm, tiles)
    weight_copy = bring(4, weight_hbm, weight_v)
    cot_copy = bring(5, cot_hbm, cot_v)
    bias_copy = bring(6, bias_hbm, bias_ref)

    pos_copy.wait()
    cnt_copy.wait()
    pos = pos_ref[...]
    lane = lax.broadcasted_iota(I32, (1, slots), 1)
    live = lane < cnt_ref[...]
    lane2 = lax.broadcasted_iota(I32, (slots, slots), 1)
    sub2 = lax.broadcasted_iota(I32, (slots, slots), 0)
    eye = lane2 == sub2
    key_f = jnp.where(live, pos, 1024 + lane)
    key_b = jnp.where(live, (pos & 15) * 64 + (pos >> 4), 1024 + lane)
    order_f, sorted_f, same_f, last_f = segment_plan(key_f, 4, eye, lane2, sub2, slots)
    order_b, sorted_b, same_b, last_b = segment_plan(key_b, 6, eye, lane2, sub2, slots)
    rb = sorted_b & 63
    rb_x, rb_z, rb_y = rb >> 4, (rb >> 3) & 1, (rb >> 1) & 3
    slot_b = jnp.where((rb & 1) == 0, (rb_y * 4 + rb_x) * 2 + rb_z, 32 + (rb_x * 4 + rb_y) * 2 + rb_z)
    for n, line in enumerate((order_f, sorted_f & 15, same_f, last_f, order_b, slot_b, same_b, last_b)):
        table_v[pl.ds(n, 1), :] = line
    table_copy = bring(7, table_v, table)
    run[slots] = jnp.zeros((blk, run.shape[2]), BF16)

    deg_copy.wait()
    feat_copy.wait()
    eye_b = lax.broadcasted_iota(I32, (blk, blk), 0) == lax.broadcasted_iota(I32, (blk, blk), 1)
    scale_row = [lax.rsqrt(deg_ref[pl.ds(b, 1), :].astype(F32)) for b in range(2)]
    scale_col = [jnp.sum(jnp.where(eye_b, s, 0.0), axis=1, keepdims=True) for s in scale_row]
    for b in range(2):
        rows = pl.ds(b * blk, blk)
        gathered[row * 2 + b] = (scale_col[b] * feat_ref[rows, :].astype(F32)).astype(BF16)

    pl.semaphore_wait(barrier, len(peers))

    slot_of, lots = {}, {}

    def arrival(key, chip=None):
        if chip is not None:
            return feat_sem.at[chip]
        return recv_sem.at[slot_of.setdefault(key, len(slot_of))]

    def send(src, dst, device, key, lot, chip=None):
        copy = pltpu.make_async_remote_copy(
            src_ref=src, dst_ref=dst, send_sem=send_sem.at[lot], recv_sem=arrival(key, chip),
            device_id=device, device_id_type=MESH,
        )
        copy.start()
        lots[lot] = lots.get(lot, 0) + 1
        return copy

    def wait_all(ref, sem):
        pltpu.make_async_copy(ref, ref, sem).wait()

    def own_pair(r):
        return gathered.at[pl.ds(r * 2, 2)]

    mine = own_pair(row)
    for other in chips:
        send(mine, mine, at_row(other * 2 + core), "feat far", 0, zl)
    send(mine, mine, sibling, "feat", 0)

    for chip in (chips[2], chips[1], chips[0]):
        wait_all(mine, arrival("feat far", chip))
        other = chip * 2 + core
        send(own_pair(other), own_pair(other), sibling, "feat", 0)
    wait_all(gathered.at[pl.ds(0, 8)], arrival("feat"))

    table_copy.wait()
    tiles_copy.wait()

    def forward(g, acc):
        steps = [g * UNROLL + u for u in range(UNROLL)]
        terms = [dot(tiles[table[0, p] & (slots - 1)], gathered[table[1, p] & 15]) for p in steps]
        for p, term in zip(steps, terms):
            acc = acc * table[2, p].astype(F32) + term
            run[p] = acc.astype(BF16)
        return acc

    zero = jnp.zeros((blk, run.shape[2]), F32)
    lax.fori_loop(0, slots // UNROLL, forward, zero)

    def ending(line, segment):
        return jnp.clip(table[line, segment], 0, slots)

    big, small = (y, x), (x, y)
    at_big, at_small = (at_y, at_x), (at_x, at_y)
    layers = (1 - zh, zh)
    both = (0, 1)
    copies = {}

    def place(n, lay):
        for h in both:
            q = step4(small[h], OFFSETS[n])
            for c in range(4):
                device = (q * 8 + c if h == 0 else c * 8 + q) + layers[lay] * 4
                part[h, c, q, layers[lay]] = run[ending(3, device * 2 + h)]

    def issue(n, lay):
        for h in both:
            q = step4(small[h], OFFSETS[n])
            for d in (2, 1, 3):
                src = part.at[h, step4(big[h], d), q, layers[lay]]
                send(src, landed.at[h, lay, n, d - 1], at_big[h](d), ("big", h, lay, n), 1 + lay)

    def finish(n, lay):
        for h in both:
            q = step4(small[h], OFFSETS[n])
            wait_all(landed.at[h, lay, n], arrival(("big", h, lay, n)))
            total = part[h, big[h], q, layers[lay]].astype(F32)
            for d in (2, 1, 3):
                total = total + landed[h, lay, n, d - 1].astype(F32)
            if n < 3:
                quarter[h, lay, n] = total.astype(BF16)
                src, dst = quarter.at[h, lay, n], landed_q.at[h, lay, n]
                send(src, dst, at_small[h](OFFSETS[n]), ("small", h, lay), 3)
            else:
                own_small[h, lay] = total

    def small_finish(lay):
        for h in both:
            wait_all(landed_q.at[h, lay], arrival(("small", h, lay)))
            total = own_small[h, lay]
            for n in range(3):
                total = total + landed_q[h, lay, n].astype(F32)
            if lay == 0:
                z_send[h] = total.astype(BF16)
                copies[h, "z"] = send(z_send.at[h], z_recv.at[h], z_peer, ("z", h), 3)
            else:
                halves[h] = total

    for n in range(4):
        place(n, 0)
        issue(n, 0)
    for n in range(4):
        place(n, 1)
    for n in range(4):
        finish(n, 0)
        issue(n, 1)
    small_finish(0)
    for n in range(4):
        finish(n, 1)
    small_finish(1)

    weight_copy.wait()
    cot_copy.wait()
    bias_copy.wait()
    weight = weight_v[...]
    bias = bias_ref[...]

    def spread(h, off, lay):
        ref = grads.at[h, big[h], step4(small[h], off), layers[lay]]
        way = RELAYED.get((off, lay))
        for d in (1, 3) if way else (2, 1, 3):
            key = ("relay", h, off, lay) if d == way else ("spread", lay)
            copies[h, off, lay, d] = send(ref, ref, at_big[h](d), key, 4 + lay)

    def relay(off, lay):
        way = RELAYED[off, lay]
        for h in both:
            copies[h, off, lay, way].wait_recv()
            ref = grads.at[h, step4(big[h], 4 - way), step4(small[h], off), layers[lay]]
            send(ref, ref, at_big[h](way), ("spread", lay), 4 + lay)

    def spread_small(h, lay):
        ref = grads.at[h, big[h], small[h], layers[lay]]
        for d in (2, 1, 3):
            copies[h, "p", lay, d] = send(ref, ref, at_small[h](d), ("pass", h, lay, d), 6)

    def pass_on(lay):
        for d in (1, 3, 2):
            for h in both:
                copies[h, "p", lay, d].wait_recv()
                spread(h, 4 - d, lay)

    for h in both:
        copies[h, "z"].wait_recv()
        hidden = scale_col[h] * (halves[h] + z_recv[h].astype(F32))
        upper, lower = two_parts(hidden)
        preact = dot(upper, weight) + dot(lower, weight) + bias
        gate = 1.0 / (1.0 + jnp.exp(-preact))
        rows = pl.ds(h * blk, blk)
        act_ref[rows, :] = (preact * gate).astype(BF16)
        grad_pre = cot_v[rows, :].astype(F32) * gate * (1.0 + preact * (1.0 - gate))
        hid_v[h] = hidden
        pre_v[h] = grad_pre
        upper, lower = two_parts(grad_pre)
        nt = ((1,), (1,))
        outgoing = scale_row[h] * (dot_general(weight, upper, nt) + dot_general(weight, lower, nt))
        grads[h, big[h], small[h], zh] = outgoing.astype(BF16)
        ref = grads.at[h, big[h], small[h], zh]
        copies[h, "g"] = send(ref, ref, z_peer, ("g", h), 3)
        spread_small(h, 1)
        spread(h, 0, 1)

    total = None
    bias_sum = None
    tn = ((0,), (0,))
    for h in both:
        hu, hl = two_parts(hid_v[h])
        gu, gl = two_parts(pre_v[h])
        term = dot_general(hu, gu, tn) + dot_general(hu, gl, tn) + dot_general(hl, gu, tn)
        sums = jnp.sum(pre_v[h], axis=0, keepdims=True)
        total = term if total is None else total + term
        bias_sum = sums if bias_sum is None else bias_sum + sums
    share = total.shape[0] // 8
    for r in range(8):
        gw_part[r % 2, r // 2, pl.ds(0, share), :] = total[r * share:(r + 1) * share, :]
        gw_part[r % 2, r // 2, pl.ds(share, 8), :] = jnp.broadcast_to(bias_sum, (8, bias_sum.shape[1]))
    gw_near = send(gw_part.at[1 - core], gw_in, sibling, "gw near", 7)

    gw_near.wait_recv()
    for z in range(4):
        gw_sum[z] = gw_part[core, z] + gw_in[z]
    gw_row[zl] = gw_sum[zl]
    for d in (1, 2, 3):
        other = step4(zl, d)
        send(gw_sum.at[other], gw_row.at[zl], at_row(other * 2 + core), "gw far", 8)
    pass_on(1)
    relay(0, 1)
    for h in both:
        copies[h, "g"].wait_recv()
        spread_small(h, 0)
        spread(h, 0, 0)
    relay(3, 1)
    relay(1, 1)
    relay(2, 1)
    wait_all(gw_row.at[pl.ds(0, 3)], arrival("gw far"))
    gw_z[zh] = gw_row[0] + gw_row[1] + gw_row[2] + gw_row[3]
    gw_across = send(gw_z.at[zh], gw_z.at[zh], z_peer, "gw z", 8)

    pass_on(0)
    relay(0, 0)

    def arrive(lay):
        relayed = sum(1 for _, other in RELAYED if other == lay)
        wait_all(tiles.at[pl.ds(0, 24 - 2 * relayed)], arrival(("spread", lay)))

    gw_across.wait_recv()
    gw_x[x] = gw_z[0] + gw_z[1]
    for d in (1, 2, 3):
        send(gw_x.at[x], gw_x.at[x], at_x(d), "gw x", 8)
    arrive(1)
    arrive(0)

    def backward(g, acc):
        steps = [g * UNROLL + u for u in range(UNROLL)]
        terms = [dot(flat_grad(table[5, p] & 63), tiles[table[4, p] & (slots - 1)]) for p in steps]
        for p, term in zip(steps, terms):
            acc = acc * table[6, p].astype(F32) + term
            run[p] = acc.astype(BF16)
        return acc

    def flat_grad(s):
        return grads[s // 32, lax.rem(s // 8, 4), lax.rem(s // 2, 4), lax.rem(s, 2)]

    zero_t = jnp.zeros((run.shape[1], blk), F32)
    middle = slots // UNROLL // 2
    acc = lax.fori_loop(0, middle, backward, zero_t)
    wait_all(gw_x.at[pl.ds(0, 3)], arrival("gw x"))
    gw_y[y] = gw_x[0] + gw_x[1] + gw_x[2] + gw_x[3]
    for d in (1, 2, 3):
        send(gw_y.at[y], gw_y.at[y], at_y(d), "gw y", 8)
    lax.fori_loop(middle, slots // UNROLL, backward, acc)
    def place_back(c, z):
        for b in range(2):
            back[c, z, b] = run[ending(7, z * 4 + c * 2 + b)]

    near = []
    for n, other in enumerate((*chips, zl)):
        place_back(1 - core, other)
        near.append(send(back.at[1 - core, other], back_in.at[n], sibling, ("back", n), 9))
    wait_all(gw_y.at[pl.ds(0, 3)], arrival("gw y"))
    piece = gw_y[0] + gw_y[1] + gw_y[2] + gw_y[3]
    gb_ref[...] = piece[share:share + 1, :]
    gw_all[row] = piece[:share, :].astype(BF16)
    mine = gw_all.at[row]
    for other in chips:
        send(mine, mine, at_row(other * 2 + core), "gw out", 10)
    send(mine, mine, sibling, "gw pass", 10)

    for other in (*chips, zl):
        place_back(core, other)
    for n, other in enumerate(chips):
        near[n].wait_recv()
        back_sum[n] = (back[core, other].astype(F32) + back_in[n].astype(F32)).astype(BF16)
        send(back_sum.at[n], back_recv.at[zl], at_row(other * 2 + core), "back", 9)
    near[3].wait_recv()
    own = back[core, zl].astype(F32) + back_in[3].astype(F32)
    wait_all(gw_all.at[pl.ds(0, 3)], arrival("gw out"))
    for chip in chips:
        passed = gw_all.at[chip * 2 + core]
        send(passed, passed, sibling, "gw pass", 10)
    wait_all(gw_all.at[pl.ds(0, 4)], arrival("gw pass"))
    for r in range(8):
        gw_ref[pl.ds(r * share, share), :] = gw_all[r].astype(F32)
    wait_all(back_recv.at[pl.ds(0, 3)], arrival("back"))
    for other in chips:
        own = own + back_recv[other].astype(F32)
    for b in range(2):
        gf_ref[pl.ds(b * blk, blk), :] = jnp.transpose(scale_row[b] * own[b]).astype(BF16)

    assert len(slot_of) == ARRIVALS
    pairs = {0, 9}
    for lot, count in lots.items():
        if lot == 7:
            ref = gw_in
        elif lot == 8:
            ref = gw_wait.at[pl.ds(0, count)]
        elif lot == 10:
            ref = gw_all.at[pl.ds(0, count)]
        else:
            ref = tiles.at[pl.ds(0, count * 2 if lot in pairs else count)]
        wait_all(ref, send_sem.at[lot])


def deliver_kernel(*refs):
    sems = refs[8]
    moves = [pltpu.make_async_copy(refs[n], refs[n + 4], sems.at[n]) for n in range(4)]
    for move in moves:
        move.start()
    for move in moves:
        move.wait()


def per_device(
    features, weight, bias_vector, cotangent, degrees, adjacency_tiles, tile_positions, tile_counts
):
    slots, blk = adjacency_tiles.shape[2:4]
    f_in, hid = weight.shape
    nodes = features.shape[0]
    share = f_in // 8
    anywhere = pl.BlockSpec(memory_space=pl.ANY)
    piece = (share + 8, hid)
    vmem = pl.BlockSpec(memory_space=pltpu.VMEM)

    def in_hbm(value):
        return pltpu.with_memory_space_constraint(value, pltpu.HBM)

    outs = pl.pallas_call(
        layer_kernel,
        out_shape=(
            pltpu.VMEM((nodes, hid), BF16),
            pltpu.VMEM((nodes, f_in), BF16),
            pltpu.VMEM((f_in, hid), F32),
            pltpu.VMEM((1, hid), F32),
        ),
        in_specs=[anywhere] * 8,
        out_specs=(vmem,) * 4,
        scratch_shapes=[
            pltpu.VMEM((nodes, f_in), BF16),
            pltpu.VMEM((1, hid), F32),
            pltpu.VMEM((2, blk), I32),
            pltpu.VMEM((1, slots), I32),
            pltpu.VMEM((1, 1), I32),
            pltpu.VMEM((slots, blk, blk), BF16),
            pltpu.VMEM((f_in, hid), BF16),
            pltpu.VMEM((nodes, hid), BF16),
            pltpu.VMEM((8, slots), I32),
            pltpu.SMEM((8, slots), I32),
            pltpu.VMEM((16, blk, f_in), BF16),
            pltpu.VMEM((slots + 1, blk, f_in), BF16),
            pltpu.VMEM((2, 4, 4, 2, blk, f_in), BF16),
            pltpu.VMEM((2, 2, 4, 3, blk, f_in), BF16),
            pltpu.VMEM((2, 2, 3, blk, f_in), BF16),
            pltpu.VMEM((2, 2, blk, f_in), F32),
            pltpu.VMEM((2, 2, 3, blk, f_in), BF16),
            pltpu.VMEM((2, blk, f_in), F32),
            pltpu.VMEM((2, blk, f_in), BF16),
            pltpu.VMEM((2, blk, f_in), BF16),
            pltpu.VMEM((2, 4, 4, 2, f_in, blk), BF16),
            pltpu.VMEM((2, blk, f_in), F32),
            pltpu.VMEM((2, blk, hid), F32),
            pltpu.VMEM((2, 4, 2, f_in, blk), BF16),
            pltpu.VMEM((4, 2, f_in, blk), BF16),
            pltpu.VMEM((3, 2, f_in, blk), BF16),
            pltpu.VMEM((4, 2, f_in, blk), BF16),
            pltpu.VMEM((2, 4) + piece, F32),
            pltpu.VMEM((4,) + piece, F32),
            pltpu.VMEM((4,) + piece, F32),
            pltpu.VMEM((4,) + piece, F32),
            pltpu.VMEM((4,) + piece, F32),
            pltpu.VMEM((4,) + piece, F32),
            pltpu.VMEM((2,) + piece, F32),
            pltpu.VMEM((8, share, hid), BF16),
            pltpu.VMEM((10,) + piece, F32),
            pltpu.SemaphoreType.DMA((9,)),
            pltpu.SemaphoreType.DMA((LOTS,)),
            pltpu.SemaphoreType.DMA((ARRIVALS,)),
            pltpu.SemaphoreType.DMA((4,)),
        ],
        compiler_params=pltpu.CompilerParams(
            collective_id=0, has_side_effects=True, vmem_limit_bytes=VMEM_BYTES
        ),
        name="graph_layer",
    )(
        in_hbm(features),
        in_hbm(weight),
        in_hbm(bias_vector.reshape(1, hid)),
        in_hbm(cotangent),
        in_hbm(degrees.reshape(2, blk)),
        in_hbm(adjacency_tiles.reshape(slots, blk, blk)),
        in_hbm(tile_positions.reshape(1, slots)),
        tile_counts,
    )
    activations, grad_features, grad_weight, grad_bias = pl.pallas_call(
        deliver_kernel,
        out_shape=tuple(pltpu.HBM(o.shape, o.dtype) for o in outs),
        in_specs=[vmem] * 4,
        out_specs=(pl.BlockSpec(memory_space=pltpu.HBM),) * 4,
        scratch_shapes=[pltpu.SemaphoreType.DMA((4,))],
        name="deliver",
    )(*(pltpu.with_memory_space_constraint(o, pltpu.VMEM) for o in outs))
    return activations, grad_features, grad_weight, grad_bias.reshape(hid)


def solution(mesh):
    placed = (
        P(("row", "col"), None),
        P(),
        P(),
        P(("row", "col"), None),
        P(("row", "col")),
        P("row", "col", None, None, None),
        P("row", "col", None),
        P("row", "col"),
    )
    return jax.shard_map(
        per_device,
        mesh=mesh,
        in_specs=placed,
        out_specs=(P(("row", "col"), None), P(("row", "col"), None), P(), P()),
        check_vma=False,
    )
```
